512 devices in a mesh: band: 32 (over y_lo, z), slab: 16 (over y_hi, x, core).
Axes of the slice: x: 4, y: 8 (y_hi: 2, y_lo: 4; y = y_hi * 4 + y_lo), z: 8, core: 2. Of those that a mesh axis runs over, the one named last changes fastest.
Arguments:
- orbitals: float32 [64, 160, 160, 128], P('band', 'slab'), may hold values from -4 to 4
- plan: int32 [32, 2, 2], replicated, may hold values from 0 to 3, all different within a row
Outputs:
- exchange: float32 [64, 160, 160, 128], P('band', 'slab')
The draws below stay inside these ranges and needn't reach their ends.
Inputs may be any that keep to these rules, and one draw needn't show every extreme that they name: Code 2 * a + c in plan[e, 0] pairs band a of block e with band c of block e - 1 (mod 32); in plan[e, 1] with band c of block e + 1. The 2 codes of one block and side are distinct.
All inputs are finite; a program needn't handle non-finite values.
Results may differ from the reference program's by a relative error of at most 0.0004.
Values sent between devices are 32-bit elements; how exact they have to be, the bound alone decides.
A program may use at most 64 MiB of HBM per device.

```python
import math
import jax
import jax.numpy as jnp
from jax import lax

NX = 128
NY = 160
NZ = 160
BAND_DEV = 2
BLOCKS = 32
BANDS = 64


def draw_orbitals(key, part):
    key = jax.random.fold_in(key, 11)
    full_shape = (BANDS, NZ, NY, NX)
    values = 0.8 * jax.random.truncated_normal(key, -5.0, 5.0, full_shape, jnp.float32)
    return values.astype(jnp.float32)


def different_ones(stream_key, rows, count, top, lift):
    sequence = jax.random.permutation(jax.random.fold_in(stream_key, 1), count)
    boost = sequence
    for power in range(3):
        boost = boost * boost // count
    boost = boost * lift // count
    chance = jax.random.randint(jax.random.fold_in(stream_key, 2), (rows, count), 0, 4096) + boost
    holders = jax.random.permutation(jax.random.fold_in(stream_key, 3), rows)[jnp.arange(count) % rows]
    chance = jnp.where(jnp.arange(rows)[:, None] == holders[None, :], 1 << 14, chance)
    merit = chance * count + jnp.arange(count)
    return lax.top_k(merit.astype(jnp.int32), top)[1].astype(jnp.int32)


def setup_inputs(seed: int = 0) -> dict:
    key_of = jax.random.split(jax.random.key(seed), 3)
    return {
        "orbitals": draw_orbitals(jax.random.fold_in(key_of[2], 71), 0),
        "plan": different_ones(key_of[1], BLOCKS * 2, BAND_DEV * BAND_DEV, BAND_DEV, 0).reshape((BLOCKS, 2, BAND_DEV)),
    }


MU_SQUARED = 0.0025
MIXING = 0.25
HIGHEST = lax.Precision.HIGHEST


def sine_table(points):
    index = jnp.arange(points, dtype=jnp.int32) + 1
    reduced = (index[:, None] * index[None, :]) % (2 * (points + 1))
    return jnp.sin(math.pi * reduced.astype(jnp.float32) / (points + 1.0))


def eigen_values(position, points):
    return 2.0 - 2.0 * jnp.cos(math.pi * (position + 1.0) / (points + 1.0))


def kernel_rows(first_row, row_count):
    along_z = eigen_values(jnp.arange(NZ, dtype=jnp.float32), NZ)
    along_y = eigen_values(jnp.arange(row_count, dtype=jnp.float32) + first_row, NY)
    along_x = eigen_values(jnp.arange(NX, dtype=jnp.float32), NX)
    factor = 32.0 * math.pi / ((NZ + 1.0) * (NY + 1.0) * (NX + 1.0))
    return factor / (along_z[:, None, None] + along_y[None, :, None] + along_x[None, None, :] + MU_SQUARED)


def screened_solve(density, table_z, table_y, table_x, kernel):
    sectioned = jnp.einsum("zyx,xk->zyk", density, table_x, precision=HIGHEST, preferred_element_type=jnp.float32)
    sectioned = jnp.einsum("zyk,yj->zjk", sectioned, table_y, precision=HIGHEST, preferred_element_type=jnp.float32)
    sectioned = jnp.einsum("zjk,zi->ijk", sectioned, table_z, precision=HIGHEST, preferred_element_type=jnp.float32) * kernel
    sectioned = jnp.einsum("ijk,iz->zjk", sectioned, table_z, precision=HIGHEST, preferred_element_type=jnp.float32)
    sectioned = jnp.einsum("zjk,jy->zyk", sectioned, table_y, precision=HIGHEST, preferred_element_type=jnp.float32)
    return jnp.einsum("zyk,kx->zyx", sectioned, table_x, precision=HIGHEST, preferred_element_type=jnp.float32)


def reference(orbitals, plan):
    blocks = plan.shape[0]
    blocked = orbitals.reshape(blocks, BAND_DEV, NZ, NY, NX)
    table_x = sine_table(NX)
    table_y = sine_table(NY)
    table_z = sine_table(NZ)
    kernel = kernel_rows(0.0, NY)
    pair_codes = jnp.arange(BAND_DEV * BAND_DEV, dtype=jnp.int32)
    right_hits = jnp.sum((plan[:, 1, :, None] == pair_codes[None, None, :]).astype(jnp.int32), axis=1)
    left_next = jnp.roll(plan[:, 0, :], -1, axis=0)
    left_hits = jnp.sum((left_next[:, :, None] == pair_codes[None, None, :]).astype(jnp.int32), axis=1)
    weights = (right_hits.reshape(blocks, BAND_DEV, BAND_DEV)
               + jnp.transpose(left_hits.reshape(blocks, BAND_DEV, BAND_DEV), (0, 2, 1))).astype(jnp.float32)

    def edge_terms(position):
        left_bands = lax.dynamic_index_in_dim(blocked, position, 0, keepdims=False)
        right_bands = lax.dynamic_index_in_dim(blocked, (position + 1) % blocks, 0, keepdims=False)
        weight = lax.dynamic_index_in_dim(weights, position, 0, keepdims=False)
        to_first = [jnp.zeros((NZ, NY, NX), jnp.float32) for _ in range(BAND_DEV)]
        to_second = [jnp.zeros((NZ, NY, NX), jnp.float32) for _ in range(BAND_DEV)]
        for left_band in range(BAND_DEV):
            for right_band in range(BAND_DEV):
                density = left_bands[left_band] * right_bands[right_band]
                potential = screened_solve(density, table_z, table_y, table_x, kernel)
                weighted = potential * weight[left_band, right_band]
                to_first[left_band] = to_first[left_band] + weighted * right_bands[right_band]
                to_second[right_band] = to_second[right_band] + weighted * left_bands[left_band]
        return jnp.stack(to_first), jnp.stack(to_second)

    carried_start = edge_terms(jnp.int32(blocks - 1))[1]

    def advance(carried, position):
        to_first, to_second = edge_terms(position)
        block_out = -MIXING * (to_first + carried)
        return to_second, block_out

    _, blocks_out = lax.scan(advance, carried_start, jnp.arange(blocks, dtype=jnp.int32))
    return blocks_out.reshape(orbitals.shape)
```

```python
import functools
import math

import jax
import jax.numpy as jnp
import ml_dtypes
import numpy as np
from jax import lax
from jax.experimental import pallas as pl
from jax.experimental.pallas import tpu as pltpu
from jax.sharding import PartitionSpec as P

MU_SQUARED = 0.0025
MIXING = 0.25
CORES = 2
HALVES = 2
GROUP = 2
MESH = pl.DeviceIdType.MESH


def split_table(table):
    high = table.astype(ml_dtypes.bfloat16)
    low = (table - high.astype(np.float64)).astype(ml_dtypes.bfloat16)
    return high, low


def sine_table(points):
    index = np.arange(points, dtype=np.int64) + 1
    reduced = (index[:, None] * index[None, :]) % (2 * (points + 1))
    return np.sin(math.pi * reduced / (points + 1.0))


def eigen_values(points):
    return 2.0 - 2.0 * np.cos(math.pi * (np.arange(points) + 1.0) / (points + 1.0))


def constants(planes, total_planes, rows, points):
    high, low = split_table(sine_table(points))
    along_x = np.block([[high, low], [high, low]])
    high, low = split_table(sine_table(rows))
    along_y = np.concatenate([high, low], axis=0)
    shift = eigen_values(rows)[:, None] + eigen_values(points)[None, :] + MU_SQUARED
    root = np.sqrt(shift + shift * shift / 4.0)
    decay = 1.0 / (1.0 + shift / 2.0 + root)
    factor = 32.0 * math.pi / ((total_planes + 1.0) * (rows + 1.0) * (points + 1.0))
    scale = factor * (total_planes + 1.0) / 2.0 / (2.0 * root)
    modes = np.stack(
        [
            decay,
            decay**planes,
            decay ** (total_planes // 2),
            decay ** (total_planes + 1),
            1.0 / (1.0 - decay ** (2 * (total_planes + 1))),
            scale,
        ]
    ).astype(np.float32)
    return along_x, along_y, modes


def halves(block):
    high = block.astype(jnp.bfloat16)
    low = (block - high.astype(jnp.float32)).astype(jnp.bfloat16)
    return jnp.concatenate([high, low], axis=1)


def times_x(block, table):
    width = block.shape[1]
    product = jnp.dot(halves(block), table, preferred_element_type=jnp.float32)
    return product[:, :width] + product[:, width:]


def times_y(table, block):
    rows, width = block.shape
    product = jnp.dot(table, halves(block), preferred_element_type=jnp.float32)
    return (product[:rows, :width] + product[rows:, :width]) + (
        product[:rows, width:] + product[rows:, width:]
    )


def kernel(
    bands, slabs, plan, own, along_x, along_y, modes, out,
    part, field, given, taken, to_owner, at_owner, from_owner, at_member, mine, other,
    in_send, in_recv, owner_send, owner_recv, half_send, half_recv,
    member_send, member_recv, out_send, out_recv,
):
    band_dev, planes, rows, _ = own.shape
    members = slabs // HALVES
    chunk = band_dev * rows // members
    per_field = rows // chunk
    groups = planes // GROUP

    band = lax.axis_index("band")
    slab = lax.axis_index("slab")
    core = lax.rem(slab, CORES)
    half = slab // members
    me = lax.rem(slab, members)

    ahead = lax.rem(band + 1, bands)
    behind = lax.rem(band + bands - 1, bands)
    partner = jnp.where(core == 0, ahead, behind)
    giver = jnp.where(core == 0, behind, ahead)
    partner_id = {"band": partner, "slab": slab}
    giver_id = {"band": giver, "slab": slab}
    across_id = {"band": band, "slab": lax.rem(slab + members, slabs)}

    def member_id(member):
        same = lax.rem(member, CORES) == core
        return {"band": jnp.where(same, band, partner), "slab": half * members + member}

    barrier = pltpu.get_barrier_semaphore()
    everyone = [partner_id, giver_id, across_id]
    everyone += [member_id(lax.rem(me + k, members)) for k in range(1, members)]
    for device in everyone:
        pl.semaphore_signal(barrier, inc=1, device_id=device, device_id_type=MESH)
    pl.semaphore_wait(barrier, len(everyone))

    def remote(source, target, send, recv, device):
        return pltpu.make_async_remote_copy(
            src_ref=source, dst_ref=target, send_sem=send, recv_sem=recv,
            device_id=device, device_id_type=MESH,
        )

    def in_copy(c, g):
        span = pl.ds(g * GROUP, GROUP)
        return remote(
            own.at[c, span], part.at[c, span], in_send.at[c, g], in_recv.at[c, g], giver_id
        )

    def out_copy(c, g):
        span = pl.ds(g * GROUP, GROUP)
        return remote(
            given.at[c, span], taken.at[c, span], out_send.at[c, g], out_recv.at[c, g], partner_id
        )

    def owner_copy(c, k, slot):
        target = lax.rem(me + k, members)
        return remote(
            to_owner.at[c, target], at_owner.at[c, slot],
            owner_send.at[c, k], owner_recv.at[c, k], member_id(target),
        )

    def member_copy(c, k, slot):
        target = lax.rem(me + k, members)
        return remote(
            from_owner.at[c, target], at_member.at[c, slot],
            member_send.at[c, k], member_recv.at[c, k], member_id(target),
        )

    def half_copy(c):
        return remote(mine.at[c], other.at[c], half_send.at[c], half_recv.at[c], across_id)

    for c in range(band_dev):
        for g in range(groups):
            in_copy(c, g).start()

    edge = jnp.where(core == 0, band, behind)
    after = lax.rem(edge + 1, bands)

    def pair(a, c):
        return jnp.where(core == 0, a, c), jnp.where(core == 0, c, a)

    def weight(a, c):
        first, second = pair(a, c)
        total = jnp.float32(0.0)
        for slot in range(band_dev):
            total += jnp.where(plan[edge, 1, slot] == band_dev * first + second, 1.0, 0.0)
            total += jnp.where(plan[after, 0, slot] == band_dev * second + first, 1.0, 0.0)
        return -MIXING * total

    weights = [[weight(a, c) for c in range(band_dev)] for a in range(band_dev)]

    def forward(c, g):
        in_copy(c, g).wait_recv()
        for step in range(GROUP):
            z = g * GROUP + step
            for a in range(band_dev):
                density = own[a, z] * part[c, z]
                x, y = pair(a, c)
                field[x, y, z] = times_y(along_y[...], times_x(density, along_x[...]))

    def summarise(c):
        def body(m, _):
            a = m // per_field
            span = pl.ds(pl.multiple_of(lax.rem(m, per_field) * chunk, 8), chunk)
            decay = modes[0, span]
            rising = field[c, a, 0, span]
            falling = field[c, a, planes - 1, span]
            for z in range(1, planes):
                rising = rising * decay + field[c, a, z, span]
                falling = falling * decay + field[c, a, planes - 1 - z, span]
            to_owner[c, m, 0] = rising
            to_owner[c, m, 1] = falling * decay
            return 0

        lax.fori_loop(0, members, body, 0)
        for k in range(1, members):
            owner_copy(c, k, me).start()
        at_owner[c, me] = to_owner[c, me]

    my_rows = pl.ds(pl.multiple_of(lax.rem(me, per_field) * chunk, 8), chunk)

    def combine(c):
        for k in range(1, members):
            owner_copy(c, k, lax.rem(me + members - k, members)).wait_recv()
        block_decay = modes[1, my_rows]
        rising = at_owner[c, 0, 0]
        falling = at_owner[c, members - 1, 1]
        for d in range(1, members):
            rising = rising * block_decay + at_owner[c, d, 0]
            falling = falling * block_decay + at_owner[c, members - 1 - d, 1]
        mine[c, 0] = rising
        mine[c, 1] = falling
        half_copy(c).start()

    def resolve(c):
        half_copy(c).wait_recv()
        decay, block_decay, half_decay = modes[0, my_rows], modes[1, my_rows], modes[2, my_rows]
        whole_decay, image = modes[3, my_rows], modes[4, my_rows]
        lower = half == 0
        rising_low = jnp.where(lower, mine[c, 0], other[c, 0])
        rising_up = jnp.where(lower, other[c, 0], mine[c, 0])
        falling_low = jnp.where(lower, mine[c, 1], other[c, 1])
        falling_up = jnp.where(lower, other[c, 1], mine[c, 1])
        at_start = falling_low + half_decay * falling_up
        at_end = decay * (rising_up + half_decay * rising_low)
        from_start = (whole_decay * at_end - at_start) * image
        from_end = decay * ((whole_decay * at_start - at_end) * image)
        rising = jnp.where(lower, from_start, half_decay * from_start + rising_low)
        falling = jnp.where(lower, half_decay * from_end + falling_up, from_end)
        for d in range(members):
            from_owner[c, d, 0] = rising
            from_owner[c, members - 1 - d, 1] = falling
            rising = rising * block_decay + at_owner[c, d, 0]
            falling = falling * block_decay + at_owner[c, members - 1 - d, 1]
        for k in range(1, members):
            member_copy(c, k, me).start()
        at_member[c, me] = from_owner[c, me]

    def solve(c):
        for k in range(1, members):
            member_copy(c, k, lax.rem(me + members - k, members)).wait_recv()

        def body(m, _):
            a = m // per_field
            for part_row in range(0, chunk, 8):
                span = pl.ds(pl.multiple_of(lax.rem(m, per_field) * chunk + part_row, 8), 8)
                decay, scale = modes[0, span], modes[5, span]
                source = [field[c, a, z, span] for z in range(planes)]
                falling = [None] * planes
                falling[planes - 1] = at_member[c, m, 1, pl.ds(part_row, 8)]
                for z in range(planes - 1, 0, -1):
                    falling[z - 1] = (falling[z] + source[z]) * decay
                rising = at_member[c, m, 0, pl.ds(part_row, 8)]
                for z in range(planes):
                    rising = rising * decay + source[z]
                    field[c, a, z, span] = (rising + falling[z]) * scale
            return 0

        lax.fori_loop(0, members, body, 0)

    def inverse(c, g):
        for step in range(GROUP):
            z = g * GROUP + step
            total = None
            for a in range(band_dev):
                x, y = pair(a, c)
                potential = times_x(times_y(along_y[...], field[x, y, z]), along_x[...])
                potential = potential * weights[a][c]
                term = potential * own[a, z]
                total = term if total is None else total + term
                mutual = potential * part[c, z]
                out[a, z] = mutual if c == 0 else out[a, z] + mutual
            given[c, z] = total
        out_copy(c, g).start()

    def loop(first, last, body):
        def step(g, _):
            body(g)
            return 0

        lax.fori_loop(first, last, step, 0)

    for c in range(band_dev):
        loop(0, groups, functools.partial(forward, c))
    for step in (summarise, combine, resolve, solve):
        for x in range(band_dev):
            step(x)
    for c in range(band_dev):
        loop(0, groups, functools.partial(inverse, c))

    def finish(c, g):
        out_copy(c, g).wait_recv()
        for step in range(GROUP):
            z = g * GROUP + step
            out[c, z] = out[c, z] + taken[c, z]

    for c in range(band_dev):
        loop(0, groups, functools.partial(finish, c))
    for c in range(band_dev):
        for g in range(groups):
            in_copy(c, g).wait_send()
            out_copy(c, g).wait_send()
        for k in range(1, members):
            owner_copy(c, k, me).wait_send()
            member_copy(c, k, me).wait_send()
        half_copy(c).wait_send()


def solution(mesh):
    bands, slabs = mesh.shape["band"], mesh.shape["slab"]

    def local(orbitals, plan):
        band_dev, planes, rows, points = orbitals.shape
        members = slabs // HALVES
        chunk = band_dev * rows // members
        groups = planes // GROUP
        along_x, along_y, modes = constants(planes, planes * slabs, rows, points)
        vmem = pl.BlockSpec(memory_space=pltpu.VMEM)
        f32 = jnp.float32
        field = pltpu.VMEM((band_dev, planes, rows, points), f32)
        exchanged = pltpu.VMEM((band_dev, members, 2, chunk, points), f32)
        return pl.pallas_call(
            functools.partial(kernel, bands, slabs),
            out_shape=jax.ShapeDtypeStruct(orbitals.shape, f32),
            in_specs=[pl.BlockSpec(memory_space=pltpu.SMEM)] + [vmem] * 4,
            out_specs=vmem,
            scratch_shapes=[
                field,
                pltpu.VMEM((band_dev, band_dev, planes, rows, points), f32),
                field,
                field,
                exchanged,
                exchanged,
                exchanged,
                exchanged,
                pltpu.VMEM((band_dev, 2, chunk, points), f32),
                pltpu.VMEM((band_dev, 2, chunk, points), f32),
                pltpu.SemaphoreType.DMA((band_dev, groups)),
                pltpu.SemaphoreType.DMA((band_dev, groups)),
                pltpu.SemaphoreType.DMA((band_dev, members)),
                pltpu.SemaphoreType.DMA((band_dev, members)),
                pltpu.SemaphoreType.DMA((band_dev,)),
                pltpu.SemaphoreType.DMA((band_dev,)),
                pltpu.SemaphoreType.DMA((band_dev, members)),
                pltpu.SemaphoreType.DMA((band_dev, members)),
                pltpu.SemaphoreType.DMA((band_dev, groups)),
                pltpu.SemaphoreType.DMA((band_dev, groups)),
            ],
            compiler_params=pltpu.CompilerParams(
                collective_id=0, has_side_effects=True, vmem_limit_bytes=48 * 2**20
            ),
            name="exchange",
        )(plan, orbitals, jnp.asarray(along_x), jnp.asarray(along_y), jnp.asarray(modes))

    in_specs = (P("band", "slab", None, None), P())
    out_specs = P("band", "slab", None, None)
    return jax.shard_map(local, mesh=mesh, in_specs=in_specs, out_specs=out_specs, check_vma=False)
```

```python
import functools
import math

import jax
import jax.numpy as jnp
import numpy as np
from jax import lax
from jax.experimental import pallas as pl
from jax.experimental.pallas import tpu as pltpu
from jax.sharding import PartitionSpec as P

MU_SQUARED = 0.0025
MIXING = 0.25
CORES = 2
HALVES = 2
GROUP = 2
MESH = pl.DeviceIdType.MESH


def sine_table(points):
    index = np.arange(points, dtype=np.int64) + 1
    reduced = (index[:, None] * index[None, :]) % (2 * (points + 1))
    return np.sin(math.pi * reduced / (points + 1.0))


def eigen_values(points):
    return 2.0 - 2.0 * np.cos(math.pi * (np.arange(points) + 1.0) / (points + 1.0))


def constants(planes, total_planes, rows, points):
    table_x = sine_table(points).astype(np.float32)
    table_y = sine_table(rows).astype(np.float32)
    shift = eigen_values(rows)[:, None] + eigen_values(points)[None, :] + MU_SQUARED
    root = np.sqrt(shift + shift * shift / 4.0)
    decay = 1.0 / (1.0 + shift / 2.0 + root)
    factor = 32.0 * math.pi / ((total_planes + 1.0) * (rows + 1.0) * (points + 1.0))
    scale = factor * (total_planes + 1.0) / 2.0 / (2.0 * root)
    modes = np.stack(
        [
            decay,
            decay**planes,
            decay ** (total_planes // 2),
            1.0 / (1.0 - decay ** (2 * (total_planes + 1))),
            scale,
        ]
    ).astype(np.float32)
    return table_x, table_y, modes


def split(block):
    high = block.astype(jnp.bfloat16)
    low = (block - high.astype(jnp.float32)).astype(jnp.bfloat16)
    return high, low


def halves(block):
    return jnp.concatenate(split(block), axis=1)


def times_x(block, table):
    width = block.shape[1]
    product = jnp.dot(halves(block), table, preferred_element_type=jnp.float32)
    return product[:, :width] + product[:, width:]


def times_y(table, block):
    rows, width = block.shape
    product = jnp.dot(table, halves(block), preferred_element_type=jnp.float32)
    return (product[:rows, :width] + product[rows:, :width]) + (
        product[:rows, width:] + product[rows:, width:]
    )


def kernel(
    bands, slabs, plan_hbm, orbitals, table_x_hbm, table_y_hbm, modes_hbm, out, taken,
    plan, own, table_x, table_y, modes, along_x, along_y,
    part, field, given, summary, at_owner, from_owner, at_member, outer, mine, other,
    load, in_send, in_recv, owner_send, owner_recv, half_send, half_recv,
    member_send, member_recv, out_send, out_recv,
):
    band_dev, planes, rows, points = own.shape
    members = slabs // HALVES
    chips = members // CORES
    chunk = rows // chips
    groups = planes // GROUP

    loads = [
        pltpu.make_async_copy(source, target, load.at[i])
        for i, (source, target) in enumerate(
            [
                (table_x_hbm, table_x),
                (table_y_hbm, table_y),
                (modes_hbm, modes),
                (plan_hbm, plan),
                (orbitals, own),
            ]
        )
    ]
    for copy in loads:
        copy.start()

    band = lax.axis_index("band")
    slab = lax.axis_index("slab")
    core = lax.rem(slab, CORES)
    half = slab // members
    me = lax.rem(slab, members)
    chip = me // CORES
    lower = half == 0

    ahead = lax.rem(band + 1, bands)
    behind = lax.rem(band + bands - 1, bands)
    partner = jnp.where(core == 0, ahead, behind)
    giver = jnp.where(core == 0, behind, ahead)
    partner_id = {"band": partner, "slab": slab}
    giver_id = {"band": giver, "slab": slab}
    across_id = {"band": band, "slab": lax.rem(slab + members, slabs)}

    def member_id(member):
        same = lax.rem(member, CORES) == core
        return {"band": jnp.where(same, band, partner), "slab": half * members + member}

    barrier = pltpu.get_barrier_semaphore()
    everyone = [partner_id, giver_id, across_id]
    everyone += [member_id(lax.rem(me + k, members)) for k in range(1, members)]
    for device in everyone:
        pl.semaphore_signal(barrier, inc=1, device_id=device, device_id_type=MESH)
    pl.semaphore_wait(barrier, len(everyone))

    def remote(source, target, send, recv, device):
        return pltpu.make_async_remote_copy(
            src_ref=source, dst_ref=target, send_sem=send, recv_sem=recv,
            device_id=device, device_id_type=MESH,
        )

    def in_copy(c, g):
        span = pl.ds(g * GROUP, GROUP)
        return remote(
            orbitals.at[c, span], part.at[c, span], in_send.at[c, g], in_recv.at[c, g], giver_id
        )

    def out_copy(c, g):
        span = pl.ds(g * GROUP, GROUP)
        return remote(
            given.at[c, span], taken.at[c, span], out_send.at[c, g], out_recv.at[c, g], partner_id
        )

    def pair(side, a, c):
        return jnp.where(side == 0, a, c), jnp.where(side == 0, c, a)

    def owner_copy(a, c, j):
        target = lax.rem(chip + j, chips)
        slot, _ = pair(core, a, c)
        return remote(
            summary.at[a, c, target], at_owner.at[slot, me], owner_send.at[a, c, j],
            owner_recv.at[slot, core ^ a ^ c, j], member_id(target * CORES + (a ^ c)),
        )

    def owner_wait(t):
        for other_core in range(CORES):
            for j in range(1 - other_core, chips):
                source = lax.rem(chip + chips - j, chips) * CORES + (core ^ other_core)
                remote(
                    summary.at[0, 0, 0], at_owner.at[t, source], owner_send.at[0, 0, j],
                    owner_recv.at[t, other_core, j], member_id(source),
                ).wait_recv()

    def member_copy(t, other_core, j):
        target = lax.rem(chip + j, chips) * CORES + (core ^ other_core)
        return remote(
            from_owner.at[t, target], at_member.at[core, t, chip],
            member_send.at[t, other_core, j], member_recv.at[core, t, j], member_id(target),
        )

    def member_wait(a, c):
        slot, _ = pair(core, a, c)
        owner = a ^ c

        def wait(j):
            source = lax.rem(chip + chips - j, chips)
            remote(
                from_owner.at[0, 0], at_member.at[owner, slot, source], member_send.at[0, 0, j],
                member_recv.at[owner, slot, j], member_id(source * CORES + owner),
            ).wait_recv()

        pl.when(core != owner)(lambda: wait(0))
        for j in range(1, chips):
            wait(j)

    def half_copy(t):
        return remote(mine.at[t], other.at[t], half_send.at[t], half_recv.at[t], across_id)

    for c in range(band_dev):
        for g in range(groups):
            in_copy(c, g).start()
    for copy in loads:
        copy.wait()
    high, low = split(table_x[...])
    for row in (0, points):
        along_x[pl.ds(row, points), pl.ds(0, points)] = high
        along_x[pl.ds(row, points), pl.ds(points, points)] = low
    high, low = split(table_y[...])
    along_y[pl.ds(0, rows)] = high
    along_y[pl.ds(rows, rows)] = low

    edge = jnp.where(core == 0, band, behind)
    after = lax.rem(edge + 1, bands)

    def weight(a, c):
        first, second = pair(core, a, c)
        total = jnp.float32(0.0)
        for slot in range(band_dev):
            total += jnp.where(plan[1, slot, edge] == band_dev * first + second, 1.0, 0.0)
            total += jnp.where(plan[0, slot, after] == band_dev * second + first, 1.0, 0.0)
        return -MIXING * total

    weights = [[weight(a, c) for c in range(band_dev)] for a in range(band_dev)]

    def forward(c, g):
        in_copy(c, g).wait_recv()
        for step in range(GROUP):
            z = g * GROUP + step
            for a in range(band_dev):
                density = own[a, z] * part[c, z]
                field[c, a, z] = times_y(along_y[...], times_x(density, along_x[...]))

    def summarise(a, c):
        def body(i, _):
            span = pl.ds(pl.multiple_of(i * chunk, 8), chunk)
            decay = modes[0, span]
            rising = field[c, a, 0, span]
            falling = field[c, a, planes - 1, span]
            for z in range(1, planes):
                rising = rising * decay + field[c, a, z, span]
                falling = falling * decay + field[c, a, planes - 1 - z, span]
            summary[a, c, i, 0] = rising
            summary[a, c, i, 1] = falling * decay
            return 0

        lax.fori_loop(0, chips, body, 0)
        for j in range(1, chips):
            owner_copy(a, c, j).start()
        pl.when(core != a ^ c)(lambda: owner_copy(a, c, 0).start())

        @pl.when(core == a ^ c)
        def _():
            slot, _ = pair(core, a, c)
            at_owner[slot, me] = summary[a, c, chip]

    my_rows = pl.ds(pl.multiple_of(chip * chunk, 8), chunk)

    def toward(decay):
        square = decay * decay
        return jnp.where(lower, 1.0, square), jnp.where(lower, square, 1.0)

    def combine(t):
        block_decay = modes[1, my_rows]
        rising = at_owner[t, 0, 0]
        falling = at_owner[t, members - 1, 1]
        for d in range(1, members):
            rising = rising * block_decay + at_owner[t, d, 0]
            falling = falling * block_decay + at_owner[t, members - 1 - d, 1]
        here, _ = toward(modes[0, my_rows])
        outward = jnp.where(lower, falling, rising)
        outer[t] = outward
        mine[t] = jnp.where(lower, rising, falling) - here * modes[2, my_rows] * outward
        half_copy(t).start()

    def resolve(t):
        half_copy(t).wait_recv()
        block_decay, half_decay, image = modes[1, my_rows], modes[2, my_rows], modes[3, my_rows]
        here, there = toward(modes[0, my_rows])
        inward = (other[t] - half_decay * half_decay * there * mine[t]) * image
        at_end = -here * (outer[t] + half_decay * inward)
        rising = jnp.where(lower, at_end, inward)
        falling = jnp.where(lower, inward, at_end)
        for d in range(members):
            from_owner[t, d, 0] = rising
            from_owner[t, members - 1 - d, 1] = falling
            rising = rising * block_decay + at_owner[t, d, 0]
            falling = falling * block_decay + at_owner[t, members - 1 - d, 1]
        at_member[core, t, chip] = from_owner[t, me]

    def send_back(t, other_core):
        for j in range(1 - other_core, chips):
            member_copy(t, other_core, j).start()

    def solve(c, a):
        slot, _ = pair(core, a, c)

        def body(i, _):
            for row in range(0, chunk, 8):
                span = pl.ds(pl.multiple_of(i * chunk + row, 8), 8)
                decay, scale = modes[0, span], modes[4, span]
                source = [field[c, a, z, span] for z in range(planes)]
                falling = [None] * planes
                falling[planes - 1] = at_member[a ^ c, slot, i, 1, pl.ds(row, 8)]
                for z in range(planes - 1, 0, -1):
                    falling[z - 1] = (falling[z] + source[z]) * decay
                rising = at_member[a ^ c, slot, i, 0, pl.ds(row, 8)]
                for z in range(planes):
                    rising = rising * decay + source[z]
                    field[c, a, z, span] = (rising + falling[z]) * scale
            return 0

        lax.fori_loop(0, chips, body, 0)

    def potential(c, a, z):
        return times_x(times_y(along_y[...], field[c, a, z]), along_x[...]) * weights[a][c]

    def first_potential(g):
        for step in range(GROUP):
            z = g * GROUP + step
            field[0, 0, z] = potential(0, 0, z)

    def inverse(c, g):
        for step in range(GROUP):
            z = g * GROUP + step
            total = None
            for a in range(band_dev):
                value = field[0, 0, z] if a == c == 0 else potential(c, a, z)
                term = value * own[a, z]
                total = term if total is None else total + term
                mutual = value * part[c, z]
                out[a, z] = mutual if c == 0 else out[a, z] + mutual
            given[c, z] = total
        out_copy(c, g).start()

    def loop(first, last, body):
        def step(g, _):
            body(g)
            return 0

        lax.fori_loop(first, last, step, 0)

    def settle(a, c):
        member_wait(a, c)
        solve(c, a)

    loop(0, groups, functools.partial(forward, 0))
    summarise(0, 0)
    summarise(1, 0)
    loop(0, groups - 2, functools.partial(forward, 1))

    @pl.when(core == 0)
    def _():
        owner_wait(0)
        combine(0)

    loop(groups - 2, groups - 1, functools.partial(forward, 1))

    loop(groups - 1, groups, functools.partial(forward, 1))
    summarise(0, 1)

    @pl.when(core == 0)
    def _():
        resolve(0)
        send_back(0, 0)
        send_back(0, 1)

    settle(0, 0)

    @pl.when(core == 1)
    def _():
        for t in range(band_dev):
            owner_wait(t)
            combine(t)
        summarise(1, 1)
        loop(0, groups, first_potential)
        resolve(1)
        send_back(1, 1)
        resolve(0)
        send_back(0, 0)
        send_back(1, 0)
        send_back(0, 1)

    @pl.when(core == 0)
    def _():
        loop(0, groups, first_potential)
        summarise(1, 1)
        owner_wait(1)
        combine(1)

    settle(1, 0)
    loop(0, 1, functools.partial(inverse, 0))

    @pl.when(core == 0)
    def _():
        resolve(1)
        send_back(1, 0)
        send_back(1, 1)

    loop(1, groups, functools.partial(inverse, 0))
    settle(0, 1)
    settle(1, 1)
    loop(0, groups, functools.partial(inverse, 1))

    for c in range(band_dev):
        for g in range(groups):
            in_copy(c, g).wait_send()
            out_copy(c, g).wait_send()
            out_copy(c, g).wait_recv()
        half_copy(c).wait_send()
        for a in range(band_dev):
            for j in range(1, chips):
                owner_copy(a, c, j).wait_send()
            pl.when(core != a ^ c)(owner_copy(a, c, 0).wait_send)
        for other_core in range(CORES):
            for j in range(1 - other_core, chips):
                member_copy(c, other_core, j).wait_send()


def solution(mesh):
    bands, slabs = mesh.shape["band"], mesh.shape["slab"]

    def local(orbitals, plan):
        band_dev, planes, rows, points = orbitals.shape
        members = slabs // HALVES
        chips = members // CORES
        chunk = rows // chips
        groups = planes // GROUP
        table_x, table_y, modes = constants(planes, planes * slabs, rows, points)
        plan = jnp.transpose(plan, (1, 2, 0))
        operands = (plan, orbitals, table_x, table_y, modes)
        f32 = jnp.float32
        field = pltpu.VMEM((band_dev, planes, rows, points), f32)
        edge = pltpu.VMEM((band_dev, chunk, points), f32)

        def semaphores(*shape):
            return [pltpu.SemaphoreType.DMA(shape)] * 2

        kept, taken = pl.pallas_call(
            functools.partial(kernel, bands, slabs),
            out_shape=[jax.ShapeDtypeStruct(orbitals.shape, f32)] * 2,
            in_specs=[pl.BlockSpec(memory_space=pltpu.HBM)] * 5,
            out_specs=[pl.BlockSpec(memory_space=pltpu.VMEM)] * 2,
            scratch_shapes=[
                pltpu.SMEM(plan.shape, plan.dtype),
                field,
                pltpu.VMEM(table_x.shape, f32),
                pltpu.VMEM(table_y.shape, f32),
                pltpu.VMEM(modes.shape, f32),
                pltpu.VMEM((2 * points, 2 * points), jnp.bfloat16),
                pltpu.VMEM((2 * rows, rows), jnp.bfloat16),
                field,
                pltpu.VMEM((band_dev, band_dev, planes, rows, points), f32),
                field,
                pltpu.VMEM((band_dev, band_dev, chips, 2, chunk, points), f32),
                pltpu.VMEM((band_dev, members, 2, chunk, points), f32),
                pltpu.VMEM((band_dev, members, 2, chunk, points), f32),
                pltpu.VMEM((CORES, band_dev, chips, 2, chunk, points), f32),
                edge,
                edge,
                edge,
                pltpu.SemaphoreType.DMA((5,)),
                *semaphores(band_dev, groups),
                *semaphores(band_dev, band_dev, chips),
                *semaphores(band_dev),
                *semaphores(CORES, band_dev, chips),
                *semaphores(band_dev, groups),
            ],
            compiler_params=pltpu.CompilerParams(
                collective_id=0, has_side_effects=True, vmem_limit_bytes=40 * 2**20
            ),
            name="exchange",
        )(*[pltpu.with_memory_space_constraint(jnp.asarray(x), pltpu.HBM) for x in operands])
        return kept + taken

    in_specs = (P("band", "slab", None, None), P())
    out_specs = P("band", "slab", None, None)
    return jax.shard_map(local, mesh=mesh, in_specs=in_specs, out_specs=out_specs, check_vma=False)
```

```python
import functools
import math

import jax
import jax.numpy as jnp
import numpy as np
from jax import lax
from jax.experimental import pallas as pl
from jax.experimental.pallas import tpu as pltpu
from jax.sharding import PartitionSpec as P

MU_SQUARED = 0.0025
MIXING = 0.25
CORES = 2
HALVES = 2
GROUP = 2
MESH = pl.DeviceIdType.MESH


def sine_table(points):
    index = np.arange(points, dtype=np.int64) + 1
    reduced = (index[:, None] * index[None, :]) % (2 * (points + 1))
    return np.sin(math.pi * reduced / (points + 1.0))


def eigen_values(points):
    return 2.0 - 2.0 * np.cos(math.pi * (np.arange(points) + 1.0) / (points + 1.0))


def constants(planes, total_planes, rows, points):
    table_x = sine_table(points).astype(np.float32)
    table_y = sine_table(rows).astype(np.float32)
    shift = eigen_values(rows)[:, None] + eigen_values(points)[None, :] + MU_SQUARED
    root = np.sqrt(shift + shift * shift / 4.0)
    decay = 1.0 / (1.0 + shift / 2.0 + root)
    factor = 32.0 * math.pi / ((total_planes + 1.0) * (rows + 1.0) * (points + 1.0))
    scale = factor * (total_planes + 1.0) / 2.0 / (2.0 * root)
    modes = np.stack(
        [
            decay,
            decay**planes,
            decay ** (total_planes // 2),
            1.0 / (1.0 - decay ** (2 * (total_planes + 1))),
            scale,
        ]
    ).astype(np.float32)
    return table_x, table_y, modes


def split(block):
    high = block.astype(jnp.bfloat16)
    low = (block - high.astype(jnp.float32)).astype(jnp.bfloat16)
    return high, low


def halves(block):
    return jnp.concatenate(split(block), axis=1)


def times_x(block, table):
    width = block.shape[1]
    product = jnp.dot(halves(block), table, preferred_element_type=jnp.float32)
    return product[:, :width] + product[:, width:]


def times_y(table, block):
    rows, width = block.shape
    product = jnp.dot(table, halves(block), preferred_element_type=jnp.float32)
    return (product[:rows, :width] + product[rows:, :width]) + (
        product[:rows, width:] + product[rows:, width:]
    )


def kernel(
    bands, slabs, plan_hbm, orbitals, table_x_hbm, table_y_hbm, modes_hbm, out, taken,
    plan, own, table_x, table_y, modes, along_x, along_y,
    part, field, given, summary, at_owner, from_owner, at_member, outer, mine, other,
    load, in_send, in_recv, owner_send, owner_recv, half_send, half_recv,
    member_send, member_recv, out_send, out_recv,
):
    band_dev, planes, rows, points = own.shape
    members = slabs // HALVES
    chips = members // CORES
    chunk = rows // chips
    groups = planes // GROUP

    loads = [
        pltpu.make_async_copy(source, target, load.at[i])
        for i, (source, target) in enumerate(
            [
                (table_x_hbm, table_x),
                (table_y_hbm, table_y),
                (modes_hbm, modes),
                (plan_hbm, plan),
                (orbitals, own),
            ]
        )
    ]
    for copy in loads:
        copy.start()

    band = lax.axis_index("band")
    slab = lax.axis_index("slab")
    core = lax.rem(slab, CORES)
    half = slab // members
    me = lax.rem(slab, members)
    chip = me // CORES
    lower = half == 0

    ahead = lax.rem(band + 1, bands)
    behind = lax.rem(band + bands - 1, bands)
    partner = jnp.where(core == 0, ahead, behind)
    giver = jnp.where(core == 0, behind, ahead)
    partner_id = {"band": partner, "slab": slab}
    giver_id = {"band": giver, "slab": slab}
    across_id = {"band": band, "slab": lax.rem(slab + members, slabs)}

    def member_id(member):
        same = lax.rem(member, CORES) == core
        return {"band": jnp.where(same, band, partner), "slab": half * members + member}

    barrier = pltpu.get_barrier_semaphore()
    everyone = [partner_id, giver_id, across_id]
    everyone += [member_id(lax.rem(me + k, members)) for k in range(1, members)]
    for device in everyone:
        pl.semaphore_signal(barrier, inc=1, device_id=device, device_id_type=MESH)
    pl.semaphore_wait(barrier, len(everyone))

    def remote(source, target, send, recv, device):
        return pltpu.make_async_remote_copy(
            src_ref=source, dst_ref=target, send_sem=send, recv_sem=recv,
            device_id=device, device_id_type=MESH,
        )

    def in_copy(c, g):
        span = pl.ds(g * GROUP, GROUP)
        return remote(
            orbitals.at[c, span], part.at[c, span], in_send.at[c, g], in_recv.at[c, g], giver_id
        )

    def out_copy(c, g):
        span = pl.ds(g * GROUP, GROUP)
        return remote(
            given.at[c, span], taken.at[c, span], out_send.at[c, g], out_recv.at[c, g], partner_id
        )

    def pair(side, a, c):
        return jnp.where(side == 0, a, c), jnp.where(side == 0, c, a)

    def owner_copy(a, c, j):
        target = lax.rem(chip + j, chips)
        slot, owner = pair(core, a, c)
        return remote(
            summary.at[a, c, target], at_owner.at[slot, me], owner_send.at[a, c, j],
            owner_recv.at[slot, lax.rem(core + owner, CORES), j],
            member_id(target * CORES + owner),
        )

    def owner_wait(t):
        for other_core in range(CORES):
            for j in range(1 - other_core, chips):
                source = lax.rem(chip + chips - j, chips) * CORES + lax.rem(core + other_core, CORES)
                remote(
                    summary.at[0, 0, 0], at_owner.at[t, source], owner_send.at[0, 0, j],
                    owner_recv.at[t, other_core, j], member_id(source),
                ).wait_recv()

    def member_copy(t, other_core, j):
        target = lax.rem(chip + j, chips) * CORES + lax.rem(core + other_core, CORES)
        return remote(
            from_owner.at[t, target], at_member.at[core, t, chip],
            member_send.at[t, other_core, j], member_recv.at[core, t, j], member_id(target),
        )

    def member_wait(a, c):
        slot, owner = pair(core, a, c)

        def wait(j):
            source = lax.rem(chip + chips - j, chips)
            remote(
                from_owner.at[0, 0], at_member.at[owner, slot, source], member_send.at[0, 0, j],
                member_recv.at[owner, slot, j], member_id(source * CORES + owner),
            ).wait_recv()

        pl.when(core != owner)(lambda: wait(0))
        for j in range(1, chips):
            wait(j)

    def half_copy(t):
        return remote(mine.at[t], other.at[t], half_send.at[t], half_recv.at[t], across_id)

    for c in range(band_dev):
        for g in range(groups):
            in_copy(c, g).start()
    for copy in loads:
        copy.wait()
    high, low = split(table_x[...])
    for row in (0, points):
        along_x[pl.ds(row, points), pl.ds(0, points)] = high
        along_x[pl.ds(row, points), pl.ds(points, points)] = low
    high, low = split(table_y[...])
    along_y[pl.ds(0, rows)] = high
    along_y[pl.ds(rows, rows)] = low

    edge = jnp.where(core == 0, band, behind)
    after = lax.rem(edge + 1, bands)

    def weight(a, c):
        first, second = pair(core, a, c)
        total = jnp.float32(0.0)
        for slot in range(band_dev):
            total += jnp.where(plan[1, slot, edge] == band_dev * first + second, 1.0, 0.0)
            total += jnp.where(plan[0, slot, after] == band_dev * second + first, 1.0, 0.0)
        return -MIXING * total

    weights = [[weight(a, c) for c in range(band_dev)] for a in range(band_dev)]

    def forward(c, g):
        in_copy(c, g).wait_recv()
        for step in range(GROUP):
            z = g * GROUP + step
            for a in range(band_dev):
                density = own[a, z] * part[c, z]
                field[c, a, z] = times_y(along_y[...], times_x(density, along_x[...]))

    def summarise(a, c):
        def body(i, _):
            span = pl.ds(pl.multiple_of(i * chunk, 8), chunk)
            decay = modes[0, span]
            rising = field[c, a, 0, span]
            falling = field[c, a, planes - 1, span]
            for z in range(1, planes):
                rising = rising * decay + field[c, a, z, span]
                falling = falling * decay + field[c, a, planes - 1 - z, span]
            summary[a, c, i, 0] = rising
            summary[a, c, i, 1] = falling * decay
            return 0

        lax.fori_loop(0, chips, body, 0)
        for j in range(1, chips):
            owner_copy(a, c, j).start()
        slot, owner = pair(core, a, c)
        pl.when(core != owner)(lambda: owner_copy(a, c, 0).start())

        @pl.when(core == owner)
        def _():
            at_owner[slot, me] = summary[a, c, chip]

    my_rows = pl.ds(pl.multiple_of(chip * chunk, 8), chunk)

    def toward(decay):
        square = decay * decay
        return jnp.where(lower, 1.0, square), jnp.where(lower, square, 1.0)

    def combine(t):
        block_decay = modes[1, my_rows]
        rising = at_owner[t, 0, 0]
        falling = at_owner[t, members - 1, 1]
        for d in range(1, members):
            rising = rising * block_decay + at_owner[t, d, 0]
            falling = falling * block_decay + at_owner[t, members - 1 - d, 1]
        here, _ = toward(modes[0, my_rows])
        outward = jnp.where(lower, falling, rising)
        outer[t] = outward
        mine[t] = jnp.where(lower, rising, falling) - here * modes[2, my_rows] * outward
        half_copy(t).start()

    def resolve(t):
        half_copy(t).wait_recv()
        block_decay, half_decay, image = modes[1, my_rows], modes[2, my_rows], modes[3, my_rows]
        here, there = toward(modes[0, my_rows])
        inward = (other[t] - half_decay * half_decay * there * mine[t]) * image
        at_end = -here * (outer[t] + half_decay * inward)
        rising = jnp.where(lower, at_end, inward)
        falling = jnp.where(lower, inward, at_end)
        for d in range(members):
            from_owner[t, d, 0] = rising
            from_owner[t, members - 1 - d, 1] = falling
            rising = rising * block_decay + at_owner[t, d, 0]
            falling = falling * block_decay + at_owner[t, members - 1 - d, 1]
        at_member[core, t, chip] = from_owner[t, me]

    def send_back(t, other_core):
        for j in range(1 - other_core, chips):
            member_copy(t, other_core, j).start()

    def solve(c, a):
        slot, owner = pair(core, a, c)

        def body(i, _):
            for row in range(0, chunk, 8):
                span = pl.ds(pl.multiple_of(i * chunk + row, 8), 8)
                decay, scale = modes[0, span], modes[4, span]
                source = [field[c, a, z, span] for z in range(planes)]
                falling = [None] * planes
                falling[planes - 1] = at_member[owner, slot, i, 1, pl.ds(row, 8)]
                for z in range(planes - 1, 0, -1):
                    falling[z - 1] = (falling[z] + source[z]) * decay
                rising = at_member[owner, slot, i, 0, pl.ds(row, 8)]
                for z in range(planes):
                    rising = rising * decay + source[z]
                    field[c, a, z, span] = (rising + falling[z]) * scale
            return 0

        lax.fori_loop(0, chips, body, 0)

    def potential(c, a, z):
        return times_x(times_y(along_y[...], field[c, a, z]), along_x[...]) * weights[a][c]

    def first_potential(g):
        for step in range(GROUP):
            z = g * GROUP + step
            field[0, 0, z] = potential(0, 0, z)

    def inverse(c, g):
        for step in range(GROUP):
            z = g * GROUP + step
            total = None
            for a in range(band_dev):
                value = field[0, 0, z] if a == c == 0 else potential(c, a, z)
                term = value * own[a, z]
                total = term if total is None else total + term
                mutual = value * part[c, z]
                out[a, z] = mutual if c == 0 else out[a, z] + mutual
            given[c, z] = total
        out_copy(c, g).start()

    def loop(first, last, body):
        def step(g, _):
            body(g)
            return 0

        lax.fori_loop(first, last, step, 0)

    def settle(a, c):
        member_wait(a, c)
        solve(c, a)

    late = 1 - core
    loop(0, groups, functools.partial(forward, 0))
    summarise(0, 0)
    summarise(1, 0)
    loop(0, groups - 2, functools.partial(forward, 1))

    @pl.when(core == 0)
    def _():
        owner_wait(0)
        combine(0)

    loop(groups - 2, groups, functools.partial(forward, 1))
    summarise(0, 1)

    @pl.when(core == 0)
    def _():
        resolve(0)
        send_back(0, 1)
        send_back(0, 0)

    owner_wait(late)
    combine(late)
    summarise(1, 1)
    settle(0, 0)
    loop(0, groups, first_potential)
    resolve(late)
    send_back(late, 0)
    send_back(late, 1)

    @pl.when(core == 1)
    def _():
        owner_wait(1)
        combine(1)

    settle(1, 0)
    loop(0, 1, functools.partial(inverse, 0))

    @pl.when(core == 1)
    def _():
        resolve(1)
        send_back(1, 0)
        send_back(1, 1)

    loop(1, groups, functools.partial(inverse, 0))
    settle(0, 1)
    settle(1, 1)
    loop(0, groups, functools.partial(inverse, 1))

    for c in range(band_dev):
        for g in range(groups):
            in_copy(c, g).wait_send()
            out_copy(c, g).wait_send()
            out_copy(c, g).wait_recv()
        half_copy(c).wait_send()
        for a in range(band_dev):
            for j in range(1, chips):
                owner_copy(a, c, j).wait_send()
            _, owner = pair(core, a, c)
            pl.when(core != owner)(owner_copy(a, c, 0).wait_send)
        for other_core in range(CORES):
            for j in range(1 - other_core, chips):
                member_copy(c, other_core, j).wait_send()


def solution(mesh):
    bands, slabs = mesh.shape["band"], mesh.shape["slab"]

    def local(orbitals, plan):
        band_dev, planes, rows, points = orbitals.shape
        members = slabs // HALVES
        chips = members // CORES
        chunk = rows // chips
        groups = planes // GROUP
        table_x, table_y, modes = constants(planes, planes * slabs, rows, points)
        plan = jnp.transpose(plan, (1, 2, 0))
        operands = (plan, orbitals, table_x, table_y, modes)
        f32 = jnp.float32
        field = pltpu.VMEM((band_dev, planes, rows, points), f32)
        edge = pltpu.VMEM((band_dev, chunk, points), f32)

        def semaphores(*shape):
            return [pltpu.SemaphoreType.DMA(shape)] * 2

        kept, taken = pl.pallas_call(
            functools.partial(kernel, bands, slabs),
            out_shape=[jax.ShapeDtypeStruct(orbitals.shape, f32)] * 2,
            in_specs=[pl.BlockSpec(memory_space=pltpu.HBM)] * 5,
            out_specs=[pl.BlockSpec(memory_space=pltpu.VMEM)] * 2,
            scratch_shapes=[
                pltpu.SMEM(plan.shape, plan.dtype),
                field,
                pltpu.VMEM(table_x.shape, f32),
                pltpu.VMEM(table_y.shape, f32),
                pltpu.VMEM(modes.shape, f32),
                pltpu.VMEM((2 * points, 2 * points), jnp.bfloat16),
                pltpu.VMEM((2 * rows, rows), jnp.bfloat16),
                field,
                pltpu.VMEM((band_dev, band_dev, planes, rows, points), f32),
                field,
                pltpu.VMEM((band_dev, band_dev, chips, 2, chunk, points), f32),
                pltpu.VMEM((band_dev, members, 2, chunk, points), f32),
                pltpu.VMEM((band_dev, members, 2, chunk, points), f32),
                pltpu.VMEM((CORES, band_dev, chips, 2, chunk, points), f32),
                edge,
                edge,
                edge,
                pltpu.SemaphoreType.DMA((5,)),
                *semaphores(band_dev, groups),
                *semaphores(band_dev, band_dev, chips),
                *semaphores(band_dev),
                *semaphores(CORES, band_dev, chips),
                *semaphores(band_dev, groups),
            ],
            compiler_params=pltpu.CompilerParams(
                collective_id=0, has_side_effects=True, vmem_limit_bytes=40 * 2**20
            ),
            name="exchange",
        )(*[pltpu.with_memory_space_constraint(jnp.asarray(x), pltpu.HBM) for x in operands])
        return kept + taken

    in_specs = (P("band", "slab", None, None), P())
    out_specs = P("band", "slab", None, None)
    return jax.shard_map(local, mesh=mesh, in_specs=in_specs, out_specs=out_specs, check_vma=False)
```

```python
import functools
import math

import jax
import jax.numpy as jnp
import numpy as np
from jax import lax
from jax.experimental import pallas as pl
from jax.experimental.pallas import tpu as pltpu
from jax.sharding import PartitionSpec as P

MU_SQUARED = 0.0025
MIXING = 0.25
CORES = 2
HALVES = 2
GROUP = 2
MESH = pl.DeviceIdType.MESH


def sine_table(points):
    index = np.arange(points, dtype=np.int64) + 1
    reduced = (index[:, None] * index[None, :]) % (2 * (points + 1))
    return np.sin(math.pi * reduced / (points + 1.0))


def eigen_values(points):
    return 2.0 - 2.0 * np.cos(math.pi * (np.arange(points) + 1.0) / (points + 1.0))


def constants(planes, total_planes, rows, points):
    table_x = sine_table(points).astype(np.float32)
    table_y = sine_table(rows).astype(np.float32)
    shift = eigen_values(rows)[:, None] + eigen_values(points)[None, :] + MU_SQUARED
    root = np.sqrt(shift + shift * shift / 4.0)
    decay = 1.0 / (1.0 + shift / 2.0 + root)
    factor = 32.0 * math.pi / ((total_planes + 1.0) * (rows + 1.0) * (points + 1.0))
    scale = factor * (total_planes + 1.0) / 2.0 / (2.0 * root)
    modes = np.stack(
        [
            decay,
            decay**planes,
            decay ** (total_planes // 2),
            1.0 / (1.0 - decay ** (2 * (total_planes + 1))),
            scale,
        ]
    ).astype(np.float32)
    return table_x, table_y, modes


def split(block):
    high = block.astype(jnp.bfloat16)
    low = (block - high.astype(jnp.float32)).astype(jnp.bfloat16)
    return high, low


def halves(block):
    return jnp.concatenate(split(block), axis=1)


def times_x(block, table):
    width = block.shape[1]
    product = jnp.dot(halves(block), table, preferred_element_type=jnp.float32)
    return product[:, :width] + product[:, width:]


def times_y(table, block):
    rows, width = block.shape
    product = jnp.dot(table, halves(block), preferred_element_type=jnp.float32)
    return (product[:rows, :width] + product[rows:, :width]) + (
        product[:rows, width:] + product[rows:, width:]
    )


def kernel(
    bands, slabs, plan_hbm, orbitals, table_x_hbm, table_y_hbm, modes_hbm, out, taken,
    plan, own, table_x, table_y, modes, along_x, along_y,
    part, field, given, summary, at_owner, from_owner, at_member, outer, mine, other,
    load, in_send, in_recv, owner_send, owner_recv, half_send, half_recv,
    member_send, member_recv, out_send, out_recv,
):
    band_dev, planes, rows, points = own.shape
    members = slabs // HALVES
    chips = members // CORES
    chunk = rows // chips
    groups = planes // GROUP

    loads = [
        pltpu.make_async_copy(source, target, load.at[i])
        for i, (source, target) in enumerate(
            [
                (table_x_hbm, table_x),
                (table_y_hbm, table_y),
                (modes_hbm, modes),
                (plan_hbm, plan),
                (orbitals, own),
            ]
        )
    ]
    for copy in loads:
        copy.start()

    band = lax.axis_index("band")
    slab = lax.axis_index("slab")
    core = lax.rem(slab, CORES)
    half = slab // members
    me = lax.rem(slab, members)
    chip = me // CORES
    lower = half == 0

    ahead = lax.rem(band + 1, bands)
    behind = lax.rem(band + bands - 1, bands)
    partner = jnp.where(core == 0, ahead, behind)
    giver = jnp.where(core == 0, behind, ahead)
    partner_id = {"band": partner, "slab": slab}
    giver_id = {"band": giver, "slab": slab}
    across_id = {"band": band, "slab": lax.rem(slab + members, slabs)}

    def member_id(member):
        same = lax.rem(member, CORES) == core
        return {"band": jnp.where(same, band, partner), "slab": half * members + member}

    barrier = pltpu.get_barrier_semaphore()
    everyone = [partner_id, giver_id, across_id]
    everyone += [member_id(lax.rem(me + k, members)) for k in range(1, members)]
    for device in everyone:
        pl.semaphore_signal(barrier, inc=1, device_id=device, device_id_type=MESH)
    pl.semaphore_wait(barrier, len(everyone))

    def remote(source, target, send, recv, device):
        return pltpu.make_async_remote_copy(
            src_ref=source, dst_ref=target, send_sem=send, recv_sem=recv,
            device_id=device, device_id_type=MESH,
        )

    def in_copy(c, g):
        span = pl.ds(g * GROUP, GROUP)
        return remote(
            orbitals.at[c, span], part.at[c, span], in_send.at[c, g], in_recv.at[c, g], giver_id
        )

    def out_copy(c, g):
        span = pl.ds(g * GROUP, GROUP)
        return remote(
            given.at[c, span], taken.at[c, span], out_send.at[c, g], out_recv.at[c, g], partner_id
        )

    def pair(side, a, c):
        return jnp.where(side == 0, a, c), jnp.where(side == 0, c, a)

    def owner_copy(a, c, j):
        target = lax.rem(chip + j, chips)
        slot, owner = pair(core, a, c)
        return remote(
            summary.at[a, c, target], at_owner.at[slot, me], owner_send.at[a, c, j],
            owner_recv.at[slot, lax.rem(core + owner, CORES), j],
            member_id(target * CORES + owner),
        )

    def owner_wait(t):
        for other_core in range(CORES):
            for j in range(1 - other_core, chips):
                source = lax.rem(chip + chips - j, chips) * CORES + lax.rem(core + other_core, CORES)
                remote(
                    summary.at[0, 0, 0], at_owner.at[t, source], owner_send.at[0, 0, j],
                    owner_recv.at[t, other_core, j], member_id(source),
                ).wait_recv()

    def member_copy(t, other_core, j):
        target = lax.rem(chip + j, chips) * CORES + lax.rem(core + other_core, CORES)
        return remote(
            from_owner.at[t, target], at_member.at[core, t, chip],
            member_send.at[t, other_core, j], member_recv.at[core, t, j], member_id(target),
        )

    def member_wait(a, c):
        slot, owner = pair(core, a, c)

        def wait(j):
            source = lax.rem(chip + chips - j, chips)
            remote(
                from_owner.at[0, 0], at_member.at[owner, slot, source], member_send.at[0, 0, j],
                member_recv.at[owner, slot, j], member_id(source * CORES + owner),
            ).wait_recv()

        pl.when(core != owner)(lambda: wait(0))
        for j in range(1, chips):
            wait(j)

    def half_copy(t):
        return remote(mine.at[t], other.at[t], half_send.at[t], half_recv.at[t], across_id)

    for c in range(band_dev):
        for g in range(groups):
            in_copy(c, g).start()
    for copy in loads:
        copy.wait()
    high, low = split(table_x[...])
    for row in (0, points):
        along_x[pl.ds(row, points), pl.ds(0, points)] = high
        along_x[pl.ds(row, points), pl.ds(points, points)] = low
    high, low = split(table_y[...])
    along_y[pl.ds(0, rows)] = high
    along_y[pl.ds(rows, rows)] = low

    edge = jnp.where(core == 0, band, behind)
    after = lax.rem(edge + 1, bands)

    def weight(a, c):
        first, second = pair(core, a, c)
        total = jnp.float32(0.0)
        for slot in range(band_dev):
            total += jnp.where(plan[1, slot, edge] == band_dev * first + second, 1.0, 0.0)
            total += jnp.where(plan[0, slot, after] == band_dev * second + first, 1.0, 0.0)
        return -MIXING * total

    weights = [[weight(a, c) for c in range(band_dev)] for a in range(band_dev)]

    def forward(c, g):
        in_copy(c, g).wait_recv()
        for step in range(GROUP):
            z = g * GROUP + step
            for a in range(band_dev):
                density = own[a, z] * part[c, z]
                field[c, a, z] = times_y(along_y[...], times_x(density, along_x[...]))

    def summarise(a, c):
        def body(i, _):
            span = pl.ds(pl.multiple_of(i * chunk, 8), chunk)
            decay = modes[0, span]
            rising = field[c, a, 0, span]
            falling = field[c, a, planes - 1, span]
            for z in range(1, planes):
                rising = rising * decay + field[c, a, z, span]
                falling = falling * decay + field[c, a, planes - 1 - z, span]
            summary[a, c, i, 0] = rising
            summary[a, c, i, 1] = falling * decay
            return 0

        lax.fori_loop(0, chips, body, 0)
        for j in range(1, chips):
            owner_copy(a, c, j).start()
        slot, owner = pair(core, a, c)
        pl.when(core != owner)(lambda: owner_copy(a, c, 0).start())

        @pl.when(core == owner)
        def _():
            at_owner[slot, me] = summary[a, c, chip]

    my_rows = pl.ds(pl.multiple_of(chip * chunk, 8), chunk)

    def toward(decay):
        square = decay * decay
        return jnp.where(lower, 1.0, square), jnp.where(lower, square, 1.0)

    def combine(t):
        block_decay = modes[1, my_rows]
        rising = at_owner[t, 0, 0]
        falling = at_owner[t, members - 1, 1]
        for d in range(1, members):
            rising = rising * block_decay + at_owner[t, d, 0]
            falling = falling * block_decay + at_owner[t, members - 1 - d, 1]
        here, _ = toward(modes[0, my_rows])
        outward = jnp.where(lower, falling, rising)
        outer[t] = outward
        mine[t] = jnp.where(lower, rising, falling) - here * modes[2, my_rows] * outward
        half_copy(t).start()

    def resolve(t):
        half_copy(t).wait_recv()
        block_decay, half_decay, image = modes[1, my_rows], modes[2, my_rows], modes[3, my_rows]
        here, there = toward(modes[0, my_rows])
        inward = (other[t] - half_decay * half_decay * there * mine[t]) * image
        at_end = -here * (outer[t] + half_decay * inward)
        rising = jnp.where(lower, at_end, inward)
        falling = jnp.where(lower, inward, at_end)
        for d in range(members):
            from_owner[t, d, 0] = rising
            from_owner[t, members - 1 - d, 1] = falling
            rising = rising * block_decay + at_owner[t, d, 0]
            falling = falling * block_decay + at_owner[t, members - 1 - d, 1]
        at_member[core, t, chip] = from_owner[t, me]

    def send_back(t, other_core):
        for j in range(1 - other_core, chips):
            member_copy(t, other_core, j).start()

    def solve(c, a):
        slot, owner = pair(core, a, c)

        def body(i, _):
            for row in range(0, chunk, 8):
                span = pl.ds(pl.multiple_of(i * chunk + row, 8), 8)
                decay, scale = modes[0, span], modes[4, span]
                source = [field[c, a, z, span] for z in range(planes)]
                falling = [None] * planes
                falling[planes - 1] = at_member[owner, slot, i, 1, pl.ds(row, 8)]
                for z in range(planes - 1, 0, -1):
                    falling[z - 1] = (falling[z] + source[z]) * decay
                rising = at_member[owner, slot, i, 0, pl.ds(row, 8)]
                for z in range(planes):
                    rising = rising * decay + source[z]
                    field[c, a, z, span] = (rising + falling[z]) * scale
            return 0

        lax.fori_loop(0, chips, body, 0)

    def potential(c, a, z):
        return times_x(times_y(along_y[...], field[c, a, z]), along_x[...]) * weights[a][c]

    def first_potential(c, g):
        for step in range(GROUP):
            z = g * GROUP + step
            field[c, 0, z] = potential(c, 0, z)

    def inverse(c, g):
        for step in range(GROUP):
            z = g * GROUP + step
            total = None
            for a in range(band_dev):
                value = field[c, 0, z] if a == 0 else potential(c, a, z)
                term = value * own[a, z]
                total = term if total is None else total + term
                mutual = value * part[c, z]
                out[a, z] = mutual if c == 0 else out[a, z] + mutual
            given[c, z] = total
        out_copy(c, g).start()

    def loop(first, last, body):
        def step(g, _):
            body(g)
            return 0

        lax.fori_loop(first, last, step, 0)

    def settle(a, c):
        member_wait(a, c)
        solve(c, a)

    late = 1 - core
    loop(0, groups, functools.partial(forward, 0))
    summarise(0, 0)
    summarise(1, 0)
    loop(0, groups - 2, functools.partial(forward, 1))

    @pl.when(core == 0)
    def _():
        owner_wait(0)
        combine(0)

    loop(groups - 2, groups, functools.partial(forward, 1))
    summarise(0, 1)

    @pl.when(core == 0)
    def _():
        resolve(0)
        send_back(0, 1)
        send_back(0, 0)

    owner_wait(late)
    combine(late)
    summarise(1, 1)
    resolve(late)
    send_back(late, 0)
    send_back(late, 1)
    settle(0, 0)
    loop(0, groups, functools.partial(first_potential, 0))

    @pl.when(core == 1)
    def _():
        owner_wait(1)
        combine(1)

    settle(1, 0)
    loop(0, 1, functools.partial(inverse, 0))

    @pl.when(core == 1)
    def _():
        resolve(1)
        send_back(1, 0)
        send_back(1, 1)

    loop(1, groups, functools.partial(inverse, 0))
    settle(0, 1)
    loop(0, groups, functools.partial(first_potential, 1))
    settle(1, 1)
    loop(0, groups, functools.partial(inverse, 1))

    for c in range(band_dev):
        for g in range(groups):
            in_copy(c, g).wait_send()
            out_copy(c, g).wait_send()
            out_copy(c, g).wait_recv()
        half_copy(c).wait_send()
        for a in range(band_dev):
            for j in range(1, chips):
                owner_copy(a, c, j).wait_send()
            _, owner = pair(core, a, c)
            pl.when(core != owner)(owner_copy(a, c, 0).wait_send)
        for other_core in range(CORES):
            for j in range(1 - other_core, chips):
                member_copy(c, other_core, j).wait_send()


def solution(mesh):
    bands, slabs = mesh.shape["band"], mesh.shape["slab"]

    def local(orbitals, plan):
        band_dev, planes, rows, points = orbitals.shape
        members = slabs // HALVES
        chips = members // CORES
        chunk = rows // chips
        groups = planes // GROUP
        table_x, table_y, modes = constants(planes, planes * slabs, rows, points)
        plan = jnp.transpose(plan, (1, 2, 0))
        operands = (plan, orbitals, table_x, table_y, modes)
        f32 = jnp.float32
        field = pltpu.VMEM((band_dev, planes, rows, points), f32)
        edge = pltpu.VMEM((band_dev, chunk, points), f32)

        def semaphores(*shape):
            return [pltpu.SemaphoreType.DMA(shape)] * 2

        kept, taken = pl.pallas_call(
            functools.partial(kernel, bands, slabs),
            out_shape=[jax.ShapeDtypeStruct(orbitals.shape, f32)] * 2,
            in_specs=[pl.BlockSpec(memory_space=pltpu.HBM)] * 5,
            out_specs=[pl.BlockSpec(memory_space=pltpu.VMEM)] * 2,
            scratch_shapes=[
                pltpu.SMEM(plan.shape, plan.dtype),
                field,
                pltpu.VMEM(table_x.shape, f32),
                pltpu.VMEM(table_y.shape, f32),
                pltpu.VMEM(modes.shape, f32),
                pltpu.VMEM((2 * points, 2 * points), jnp.bfloat16),
                pltpu.VMEM((2 * rows, rows), jnp.bfloat16),
                field,
                pltpu.VMEM((band_dev, band_dev, planes, rows, points), f32),
                field,
                pltpu.VMEM((band_dev, band_dev, chips, 2, chunk, points), f32),
                pltpu.VMEM((band_dev, members, 2, chunk, points), f32),
                pltpu.VMEM((band_dev, members, 2, chunk, points), f32),
                pltpu.VMEM((CORES, band_dev, chips, 2, chunk, points), f32),
                edge,
                edge,
                edge,
                pltpu.SemaphoreType.DMA((5,)),
                *semaphores(band_dev, groups),
                *semaphores(band_dev, band_dev, chips),
                *semaphores(band_dev),
                *semaphores(CORES, band_dev, chips),
                *semaphores(band_dev, groups),
            ],
            compiler_params=pltpu.CompilerParams(
                collective_id=0, has_side_effects=True, vmem_limit_bytes=40 * 2**20
            ),
            name="exchange",
        )(*[pltpu.with_memory_space_constraint(jnp.asarray(x), pltpu.HBM) for x in operands])
        return kept + taken

    in_specs = (P("band", "slab", None, None), P())
    out_specs = P("band", "slab", None, None)
    return jax.shard_map(local, mesh=mesh, in_specs=in_specs, out_specs=out_specs, check_vma=False)
```

```python
import functools
import math

import jax
import jax.numpy as jnp
import numpy as np
from jax import lax
from jax.experimental import pallas as pl
from jax.experimental.pallas import tpu as pltpu
from jax.sharding import PartitionSpec as P

MU_SQUARED = 0.0025
MIXING = 0.25
CORES = 2
HALVES = 2
GROUP = 2
MESH = pl.DeviceIdType.MESH


def sine_table(points):
    index = np.arange(points, dtype=np.int64) + 1
    reduced = (index[:, None] * index[None, :]) % (2 * (points + 1))
    return np.sin(math.pi * reduced / (points + 1.0))


def eigen_values(points):
    return 2.0 - 2.0 * np.cos(math.pi * (np.arange(points) + 1.0) / (points + 1.0))


def constants(planes, total_planes, rows, points):
    table_x = sine_table(points).astype(np.float32)
    table_y = sine_table(rows).astype(np.float32)
    shift = eigen_values(rows)[:, None] + eigen_values(points)[None, :] + MU_SQUARED
    root = np.sqrt(shift + shift * shift / 4.0)
    decay = 1.0 / (1.0 + shift / 2.0 + root)
    factor = 32.0 * math.pi / ((total_planes + 1.0) * (rows + 1.0) * (points + 1.0))
    scale = factor * (total_planes + 1.0) / 2.0 / (2.0 * root)
    modes = np.stack(
        [
            decay,
            decay**planes,
            decay ** (total_planes // 2),
            1.0 / (1.0 - decay ** (2 * (total_planes + 1))),
            scale,
        ]
    ).astype(np.float32)
    return table_x, table_y, modes


def split(block):
    high = block.astype(jnp.bfloat16)
    low = (block - high.astype(jnp.float32)).astype(jnp.bfloat16)
    return high, low


def halves(block):
    return jnp.concatenate(split(block), axis=1)


def times_x(block, table):
    width = block.shape[1]
    product = jnp.dot(halves(block), table, preferred_element_type=jnp.float32)
    return product[:, :width] + product[:, width:]


def times_y(table, block):
    rows, width = block.shape
    product = jnp.dot(table, halves(block), preferred_element_type=jnp.float32)
    return (product[:rows, :width] + product[rows:, :width]) + (
        product[:rows, width:] + product[rows:, width:]
    )


def kernel(
    bands, slabs, plan_hbm, orbitals, table_x_hbm, table_y_hbm, modes_hbm, out, taken,
    plan, own, table_x, table_y, modes, along_x, along_y,
    part, field, given, summary, at_owner, from_owner, at_member, outer, mine, other,
    load, in_send, in_recv, owner_send, owner_recv, half_send, half_recv,
    member_send, member_recv, out_send, out_recv,
):
    band_dev, planes, rows, points = own.shape
    members = slabs // HALVES
    chips = members // CORES
    chunk = rows // chips
    groups = planes // GROUP

    loads = [
        pltpu.make_async_copy(source, target, load.at[i])
        for i, (source, target) in enumerate(
            [
                (table_x_hbm, table_x),
                (table_y_hbm, table_y),
                (modes_hbm, modes),
                (plan_hbm, plan),
                (orbitals, own),
            ]
        )
    ]
    for copy in loads:
        copy.start()

    band = lax.axis_index("band")
    slab = lax.axis_index("slab")
    core = lax.rem(slab, CORES)
    half = slab // members
    me = lax.rem(slab, members)
    chip = me // CORES
    lower = half == 0

    ahead = lax.rem(band + 1, bands)
    behind = lax.rem(band + bands - 1, bands)
    partner = jnp.where(core == 0, ahead, behind)
    giver = jnp.where(core == 0, behind, ahead)
    partner_id = {"band": partner, "slab": slab}
    giver_id = {"band": giver, "slab": slab}
    across_id = {"band": band, "slab": lax.rem(slab + members, slabs)}

    def member_id(member):
        same = lax.rem(member, CORES) == core
        return {"band": jnp.where(same, band, partner), "slab": half * members + member}

    barrier = pltpu.get_barrier_semaphore()
    everyone = [partner_id, giver_id, across_id]
    everyone += [member_id(lax.rem(me + k, members)) for k in range(1, members)]
    for device in everyone:
        pl.semaphore_signal(barrier, inc=1, device_id=device, device_id_type=MESH)
    pl.semaphore_wait(barrier, len(everyone))

    def remote(source, target, send, recv, device):
        return pltpu.make_async_remote_copy(
            src_ref=source, dst_ref=target, send_sem=send, recv_sem=recv,
            device_id=device, device_id_type=MESH,
        )

    def in_copy(c, g):
        span = pl.ds(g * GROUP, GROUP)
        return remote(
            orbitals.at[c, span], part.at[c, span], in_send.at[c, g], in_recv.at[c, g], giver_id
        )

    def out_copy(c, g):
        span = pl.ds(g * GROUP, GROUP)
        return remote(
            given.at[c, span], taken.at[c, span], out_send.at[c, g], out_recv.at[c, g], partner_id
        )

    def pair(side, a, c):
        return jnp.where(side == 0, a, c), jnp.where(side == 0, c, a)

    def owner_copy(a, c, j):
        target = lax.rem(chip + j, chips)
        slot, owner = pair(core, a, c)
        return remote(
            summary.at[a, c, target], at_owner.at[slot, me], owner_send.at[a, c, j],
            owner_recv.at[slot, lax.rem(core + owner, CORES), j],
            member_id(target * CORES + owner),
        )

    def owner_wait(t):
        for other_core in range(CORES):
            for j in range(1 - other_core, chips):
                source = lax.rem(chip + chips - j, chips) * CORES + lax.rem(core + other_core, CORES)
                remote(
                    summary.at[0, 0, 0], at_owner.at[t, source], owner_send.at[0, 0, j],
                    owner_recv.at[t, other_core, j], member_id(source),
                ).wait_recv()

    def member_copy(t, other_core, j):
        target = lax.rem(chip + j, chips) * CORES + lax.rem(core + other_core, CORES)
        return remote(
            from_owner.at[t, target], at_member.at[core, t, chip],
            member_send.at[t, other_core, j], member_recv.at[core, t, j], member_id(target),
        )

    def member_wait(a, c):
        slot, owner = pair(core, a, c)

        def wait(j):
            source = lax.rem(chip + chips - j, chips)
            remote(
                from_owner.at[0, 0], at_member.at[owner, slot, source], member_send.at[0, 0, j],
                member_recv.at[owner, slot, j], member_id(source * CORES + owner),
            ).wait_recv()

        pl.when(core != owner)(lambda: wait(0))
        for j in range(1, chips):
            wait(j)

    def half_copy(t):
        return remote(mine.at[t], other.at[t], half_send.at[t], half_recv.at[t], across_id)

    for c in range(band_dev):
        for g in range(groups):
            in_copy(c, g).start()
    for copy in loads:
        copy.wait()
    high, low = split(table_x[...])
    for row in (0, points):
        along_x[pl.ds(row, points), pl.ds(0, points)] = high
        along_x[pl.ds(row, points), pl.ds(points, points)] = low
    high, low = split(table_y[...])
    along_y[pl.ds(0, rows)] = high
    along_y[pl.ds(rows, rows)] = low

    edge = jnp.where(core == 0, band, behind)
    after = lax.rem(edge + 1, bands)

    def weight(a, c):
        first, second = pair(core, a, c)
        total = jnp.float32(0.0)
        for slot in range(band_dev):
            total += jnp.where(plan[1, slot, edge] == band_dev * first + second, 1.0, 0.0)
            total += jnp.where(plan[0, slot, after] == band_dev * second + first, 1.0, 0.0)
        return -MIXING * total

    weights = [[weight(a, c) for c in range(band_dev)] for a in range(band_dev)]

    def forward(c, g):
        in_copy(c, g).wait_recv()
        for step in range(GROUP):
            z = g * GROUP + step
            for a in range(band_dev):
                density = own[a, z] * part[c, z]
                field[c, a, z] = times_y(along_y[...], times_x(density, along_x[...]))

    def summarise(a, c):
        def body(i, _):
            span = pl.ds(pl.multiple_of(i * chunk, 8), chunk)
            decay = modes[0, span]
            rising = field[c, a, 0, span]
            falling = field[c, a, planes - 1, span]
            for z in range(1, planes):
                rising = rising * decay + field[c, a, z, span]
                falling = falling * decay + field[c, a, planes - 1 - z, span]
            summary[a, c, i, 0] = rising
            summary[a, c, i, 1] = falling * decay
            return 0

        lax.fori_loop(0, chips, body, 0)
        for j in range(1, chips):
            owner_copy(a, c, j).start()
        slot, owner = pair(core, a, c)
        pl.when(core != owner)(lambda: owner_copy(a, c, 0).start())

        @pl.when(core == owner)
        def _():
            at_owner[slot, me] = summary[a, c, chip]

    my_rows = pl.ds(pl.multiple_of(chip * chunk, 8), chunk)

    def toward(decay):
        square = decay * decay
        return jnp.where(lower, 1.0, square), jnp.where(lower, square, 1.0)

    def combine(t):
        block_decay = modes[1, my_rows]
        rising = at_owner[t, 0, 0]
        falling = at_owner[t, members - 1, 1]
        for d in range(1, members):
            rising = rising * block_decay + at_owner[t, d, 0]
            falling = falling * block_decay + at_owner[t, members - 1 - d, 1]
        here, _ = toward(modes[0, my_rows])
        outward = jnp.where(lower, falling, rising)
        outer[t] = outward
        mine[t] = jnp.where(lower, rising, falling) - here * modes[2, my_rows] * outward
        half_copy(t).start()

    def resolve(t):
        half_copy(t).wait_recv()
        block_decay, half_decay, image = modes[1, my_rows], modes[2, my_rows], modes[3, my_rows]
        here, there = toward(modes[0, my_rows])
        inward = (other[t] - half_decay * half_decay * there * mine[t]) * image
        at_end = -here * (outer[t] + half_decay * inward)
        rising = jnp.where(lower, at_end, inward)
        falling = jnp.where(lower, inward, at_end)
        for d in range(members):
            from_owner[t, d, 0] = rising
            from_owner[t, members - 1 - d, 1] = falling
            rising = rising * block_decay + at_owner[t, d, 0]
            falling = falling * block_decay + at_owner[t, members - 1 - d, 1]
        at_member[core, t, chip] = from_owner[t, me]

    def send_back(t, other_core):
        for j in range(1 - other_core, chips):
            member_copy(t, other_core, j).start()

    def solve(c, a):
        slot, owner = pair(core, a, c)

        def body(i, _):
            for row in range(0, chunk, 8):
                span = pl.ds(pl.multiple_of(i * chunk + row, 8), 8)
                decay, scale = modes[0, span], modes[4, span]
                source = [field[c, a, z, span] for z in range(planes)]
                falling = [None] * planes
                falling[planes - 1] = at_member[owner, slot, i, 1, pl.ds(row, 8)]
                for z in range(planes - 1, 0, -1):
                    falling[z - 1] = (falling[z] + source[z]) * decay
                rising = at_member[owner, slot, i, 0, pl.ds(row, 8)]
                for z in range(planes):
                    rising = rising * decay + source[z]
                    field[c, a, z, span] = (rising + falling[z]) * scale
            return 0

        lax.fori_loop(0, chips, body, 0)

    def potential(c, a, z):
        return times_x(times_y(along_y[...], field[c, a, z]), along_x[...]) * weights[a][c]

    def first_potential(c, g):
        for step in range(GROUP):
            z = g * GROUP + step
            field[c, 0, z] = potential(c, 0, z)

    def inverse(c, g):
        for step in range(GROUP):
            z = g * GROUP + step
            total = None
            for a in range(band_dev):
                value = field[c, 0, z] if a == 0 else potential(c, a, z)
                term = value * own[a, z]
                total = term if total is None else total + term
                mutual = value * part[c, z]
                out[a, z] = mutual if c == 0 else out[a, z] + mutual
            given[c, z] = total
        out_copy(c, g).start()

    def loop(first, last, body):
        def step(g, _):
            body(g)
            return 0

        lax.fori_loop(first, last, step, 0)

    def settle(a, c):
        member_wait(a, c)
        solve(c, a)

    late = 1 - core
    loop(0, groups, functools.partial(forward, 0))
    summarise(0, 0)
    summarise(1, 0)
    loop(0, groups - 2, functools.partial(forward, 1))

    @pl.when(core == 0)
    def _():
        owner_wait(0)
        combine(0)

    loop(groups - 2, groups, functools.partial(forward, 1))
    summarise(0, 1)

    @pl.when(core == 0)
    def _():
        resolve(0)
        send_back(0, 1)
        send_back(0, 0)

    summarise(1, 1)
    owner_wait(late)
    combine(late)
    resolve(late)
    send_back(late, 0)
    send_back(late, 1)
    settle(0, 0)
    loop(0, groups, functools.partial(first_potential, 0))

    @pl.when(core == 1)
    def _():
        owner_wait(1)
        combine(1)

    settle(1, 0)
    loop(0, 1, functools.partial(inverse, 0))

    @pl.when(core == 1)
    def _():
        resolve(1)
        send_back(1, 0)
        send_back(1, 1)

    loop(1, groups, functools.partial(inverse, 0))
    settle(0, 1)
    loop(0, groups, functools.partial(first_potential, 1))
    settle(1, 1)
    loop(0, groups, functools.partial(inverse, 1))

    for c in range(band_dev):
        for g in range(groups):
            in_copy(c, g).wait_send()
            out_copy(c, g).wait_send()
            out_copy(c, g).wait_recv()
        half_copy(c).wait_send()
        for a in range(band_dev):
            for j in range(1, chips):
                owner_copy(a, c, j).wait_send()
            _, owner = pair(core, a, c)
            pl.when(core != owner)(owner_copy(a, c, 0).wait_send)
        for other_core in range(CORES):
            for j in range(1 - other_core, chips):
                member_copy(c, other_core, j).wait_send()


def solution(mesh):
    bands, slabs = mesh.shape["band"], mesh.shape["slab"]

    def local(orbitals, plan):
        band_dev, planes, rows, points = orbitals.shape
        members = slabs // HALVES
        chips = members // CORES
        chunk = rows // chips
        groups = planes // GROUP
        table_x, table_y, modes = constants(planes, planes * slabs, rows, points)
        plan = jnp.transpose(plan, (1, 2, 0))
        operands = (plan, orbitals, table_x, table_y, modes)
        f32 = jnp.float32
        field = pltpu.VMEM((band_dev, planes, rows, points), f32)
        edge = pltpu.VMEM((band_dev, chunk, points), f32)

        def semaphores(*shape):
            return [pltpu.SemaphoreType.DMA(shape)] * 2

        kept, taken = pl.pallas_call(
            functools.partial(kernel, bands, slabs),
            out_shape=[jax.ShapeDtypeStruct(orbitals.shape, f32)] * 2,
            in_specs=[pl.BlockSpec(memory_space=pltpu.HBM)] * 5,
            out_specs=[pl.BlockSpec(memory_space=pltpu.VMEM)] * 2,
            scratch_shapes=[
                pltpu.SMEM(plan.shape, plan.dtype),
                field,
                pltpu.VMEM(table_x.shape, f32),
                pltpu.VMEM(table_y.shape, f32),
                pltpu.VMEM(modes.shape, f32),
                pltpu.VMEM((2 * points, 2 * points), jnp.bfloat16),
                pltpu.VMEM((2 * rows, rows), jnp.bfloat16),
                field,
                pltpu.VMEM((band_dev, band_dev, planes, rows, points), f32),
                field,
                pltpu.VMEM((band_dev, band_dev, chips, 2, chunk, points), f32),
                pltpu.VMEM((band_dev, members, 2, chunk, points), f32),
                pltpu.VMEM((band_dev, members, 2, chunk, points), f32),
                pltpu.VMEM((CORES, band_dev, chips, 2, chunk, points), f32),
                edge,
                edge,
                edge,
                pltpu.SemaphoreType.DMA((5,)),
                *semaphores(band_dev, groups),
                *semaphores(band_dev, band_dev, chips),
                *semaphores(band_dev),
                *semaphores(CORES, band_dev, chips),
                *semaphores(band_dev, groups),
            ],
            compiler_params=pltpu.CompilerParams(
                collective_id=0, has_side_effects=True, vmem_limit_bytes=40 * 2**20
            ),
            name="exchange",
        )(*[pltpu.with_memory_space_constraint(jnp.asarray(x), pltpu.HBM) for x in operands])
        return kept + taken

    in_specs = (P("band", "slab", None, None), P())
    out_specs = P("band", "slab", None, None)
    return jax.shard_map(local, mesh=mesh, in_specs=in_specs, out_specs=out_specs, check_vma=False)
```

```python
import functools
import math

import jax
import jax.numpy as jnp
import numpy as np
from jax import lax
from jax.experimental import pallas as pl
from jax.experimental.pallas import tpu as pltpu
from jax.sharding import PartitionSpec as P

MU_SQUARED = 0.0025
MIXING = 0.25
CORES = 2
HALVES = 2
GROUP = 2
MESH = pl.DeviceIdType.MESH


def sine_table(points):
    index = np.arange(points, dtype=np.int64) + 1
    reduced = (index[:, None] * index[None, :]) % (2 * (points + 1))
    return np.sin(math.pi * reduced / (points + 1.0))


def eigen_values(points):
    return 2.0 - 2.0 * np.cos(math.pi * (np.arange(points) + 1.0) / (points + 1.0))


def constants(planes, total_planes, rows, points):
    table_x = sine_table(points).astype(np.float32)
    table_y = sine_table(rows).astype(np.float32)
    shift = eigen_values(rows)[:, None] + eigen_values(points)[None, :] + MU_SQUARED
    root = np.sqrt(shift + shift * shift / 4.0)
    decay = 1.0 / (1.0 + shift / 2.0 + root)
    factor = 32.0 * math.pi / ((total_planes + 1.0) * (rows + 1.0) * (points + 1.0))
    scale = factor * (total_planes + 1.0) / 2.0 / (2.0 * root)
    modes = np.stack(
        [
            decay,
            decay**planes,
            decay ** (total_planes // 2),
            1.0 / (1.0 - decay ** (2 * (total_planes + 1))),
            scale,
        ]
    ).astype(np.float32)
    return table_x, table_y, modes


def split(block):
    high = block.astype(jnp.bfloat16)
    low = (block - high.astype(jnp.float32)).astype(jnp.bfloat16)
    return high, low


def halves(block):
    return jnp.concatenate(split(block), axis=1)


def times_x(block, table):
    width = block.shape[1]
    product = jnp.dot(halves(block), table, preferred_element_type=jnp.float32)
    return product[:, :width] + product[:, width:]


def times_y(table, block):
    rows, width = block.shape
    product = jnp.dot(table, halves(block), preferred_element_type=jnp.float32)
    return (product[:rows, :width] + product[rows:, :width]) + (
        product[:rows, width:] + product[rows:, width:]
    )


def kernel(
    bands, slabs, plan_hbm, orbitals, table_x_hbm, table_y_hbm, modes_hbm, out, taken,
    plan, own, table_x, table_y, modes, along_x, along_y,
    part, field, given, summary, at_owner, from_owner, at_member, outer, mine, other,
    load, in_send, in_recv, owner_send, owner_recv, half_send, half_recv,
    member_send, member_recv, out_send, out_recv,
):
    band_dev, planes, rows, points = own.shape
    members = slabs // HALVES
    chips = members // CORES
    chunk = rows // chips
    groups = planes // GROUP
    far_first = sorted(range(1, chips), key=lambda j: -min(j, chips - j))

    band = lax.axis_index("band")
    slab = lax.axis_index("slab")
    core = lax.rem(slab, CORES)
    half = slab // members
    me = lax.rem(slab, members)
    chip = me // CORES
    lower = half == 0

    ahead = lax.rem(band + 1, bands)
    behind = lax.rem(band + bands - 1, bands)
    partner = jnp.where(core == 0, ahead, behind)
    giver = jnp.where(core == 0, behind, ahead)
    partner_id = {"band": partner, "slab": slab}
    giver_id = {"band": giver, "slab": slab}
    across_id = {"band": band, "slab": lax.rem(slab + members, slabs)}

    def member_id(member):
        same = lax.rem(member, CORES) == core
        return {"band": jnp.where(same, band, partner), "slab": half * members + member}

    barrier = pltpu.get_barrier_semaphore()
    everyone = [across_id, giver_id, partner_id]
    everyone += [member_id(lax.rem(me + k, members)) for k in range(1, members)]
    for device in everyone:
        pl.semaphore_signal(barrier, inc=1, device_id=device, device_id_type=MESH)
    loads = [
        pltpu.make_async_copy(source, target, load.at[i])
        for i, (source, target) in enumerate(
            [
                (table_x_hbm, table_x),
                (table_y_hbm, table_y),
                (modes_hbm, modes),
                (plan_hbm, plan),
                (orbitals, own),
            ]
        )
    ]
    for copy in loads:
        copy.start()

    pl.semaphore_wait(barrier, len(everyone))

    def remote(source, target, send, recv, device):
        return pltpu.make_async_remote_copy(
            src_ref=source, dst_ref=target, send_sem=send, recv_sem=recv,
            device_id=device, device_id_type=MESH,
        )

    def in_copy(c, g):
        span = pl.ds(g * GROUP, GROUP)
        return remote(
            orbitals.at[c, span], part.at[c, span], in_send.at[c, g], in_recv.at[c, g], giver_id
        )

    def out_copy(c, g):
        span = pl.ds(g * GROUP, GROUP)
        return remote(
            given.at[c, span], taken.at[c, span], out_send.at[c, g], out_recv.at[c, g], partner_id
        )

    def pair(side, a, c):
        return jnp.where(side == 0, a, c), jnp.where(side == 0, c, a)

    def owner_copy(a, c, j):
        target = lax.rem(chip + j, chips)
        slot, owner = pair(core, a, c)
        return remote(
            summary.at[a, c, target], at_owner.at[slot, me], owner_send.at[a, c, j],
            owner_recv.at[slot, lax.rem(core + owner, CORES), j],
            member_id(target * CORES + owner),
        )

    def owner_wait(t):
        for other_core in range(CORES):
            for j in range(1 - other_core, chips):
                source = lax.rem(chip + chips - j, chips) * CORES + lax.rem(core + other_core, CORES)
                remote(
                    summary.at[0, 0, 0], at_owner.at[t, source], owner_send.at[0, 0, j],
                    owner_recv.at[t, other_core, j], member_id(source),
                ).wait_recv()

    def member_copy(t, other_core, j):
        target = lax.rem(chip + j, chips) * CORES + lax.rem(core + other_core, CORES)
        return remote(
            from_owner.at[t, target], at_member.at[core, t, chip],
            member_send.at[t, other_core, j], member_recv.at[core, t, j], member_id(target),
        )

    def member_wait(a, c):
        slot, owner = pair(core, a, c)

        def wait(j):
            source = lax.rem(chip + chips - j, chips)
            remote(
                from_owner.at[0, 0], at_member.at[owner, slot, source], member_send.at[0, 0, j],
                member_recv.at[owner, slot, j], member_id(source * CORES + owner),
            ).wait_recv()

        pl.when(core != owner)(lambda: wait(0))
        for j in range(1, chips):
            wait(j)

    def half_copy(t):
        return remote(mine.at[t], other.at[t], half_send.at[t], half_recv.at[t], across_id)

    for c in range(band_dev):
        for g in range(groups):
            in_copy(c, g).start()
    for copy in loads:
        copy.wait()
    high, low = split(table_x[...])
    for row in (0, points):
        along_x[pl.ds(row, points), pl.ds(0, points)] = high
        along_x[pl.ds(row, points), pl.ds(points, points)] = low
    high, low = split(table_y[...])
    along_y[pl.ds(0, rows)] = high
    along_y[pl.ds(rows, rows)] = low

    edge = jnp.where(core == 0, band, behind)
    after = lax.rem(edge + 1, bands)

    def weight(a, c):
        first, second = pair(core, a, c)
        total = jnp.float32(0.0)
        for slot in range(band_dev):
            total += jnp.where(plan[1, slot, edge] == band_dev * first + second, 1.0, 0.0)
            total += jnp.where(plan[0, slot, after] == band_dev * second + first, 1.0, 0.0)
        return -MIXING * total

    weights = [[weight(a, c) for c in range(band_dev)] for a in range(band_dev)]

    def forward(c, g):
        in_copy(c, g).wait_recv()
        for step in range(GROUP):
            z = g * GROUP + step
            for a in range(band_dev):
                density = own[a, z] * part[c, z]
                field[c, a, z] = times_y(along_y[...], times_x(density, along_x[...]))

    def summarise(a, c):
        def body(i, _):
            span = pl.ds(pl.multiple_of(i * chunk, 8), chunk)
            decay = modes[0, span]
            rising = field[c, a, 0, span]
            falling = field[c, a, planes - 1, span]
            for z in range(1, planes):
                rising = rising * decay + field[c, a, z, span]
                falling = falling * decay + field[c, a, planes - 1 - z, span]
            summary[a, c, i, 0] = rising
            summary[a, c, i, 1] = falling * decay
            return 0

        lax.fori_loop(0, chips, body, 0)
        for j in far_first:
            owner_copy(a, c, j).start()
        slot, owner = pair(core, a, c)
        pl.when(core != owner)(lambda: owner_copy(a, c, 0).start())

        @pl.when(core == owner)
        def _():
            at_owner[slot, me] = summary[a, c, chip]

    my_rows = pl.ds(pl.multiple_of(chip * chunk, 8), chunk)

    def toward(decay):
        square = decay * decay
        return jnp.where(lower, 1.0, square), jnp.where(lower, square, 1.0)

    def combine(t):
        block_decay = modes[1, my_rows]
        rising = at_owner[t, 0, 0]
        falling = at_owner[t, members - 1, 1]
        for d in range(1, members):
            rising = rising * block_decay + at_owner[t, d, 0]
            falling = falling * block_decay + at_owner[t, members - 1 - d, 1]
        here, _ = toward(modes[0, my_rows])
        outward = jnp.where(lower, falling, rising)
        outer[t] = outward
        mine[t] = jnp.where(lower, rising, falling) - here * modes[2, my_rows] * outward
        half_copy(t).start()

    def resolve(t):
        half_copy(t).wait_recv()
        block_decay, half_decay, image = modes[1, my_rows], modes[2, my_rows], modes[3, my_rows]
        here, there = toward(modes[0, my_rows])
        inward = (other[t] - half_decay * half_decay * there * mine[t]) * image
        at_end = -here * (outer[t] + half_decay * inward)
        rising = jnp.where(lower, at_end, inward)
        falling = jnp.where(lower, inward, at_end)
        for d in range(members):
            from_owner[t, d, 0] = rising
            from_owner[t, members - 1 - d, 1] = falling
            rising = rising * block_decay + at_owner[t, d, 0]
            falling = falling * block_decay + at_owner[t, members - 1 - d, 1]
        at_member[core, t, chip] = from_owner[t, me]

    def send_back(t, other_core):
        for j in far_first + [0] * other_core:
            member_copy(t, other_core, j).start()

    def solve(c, a):
        slot, owner = pair(core, a, c)

        def body(i, _):
            for row in range(0, chunk, 8):
                span = pl.ds(pl.multiple_of(i * chunk + row, 8), 8)
                decay, scale = modes[0, span], modes[4, span]
                source = [field[c, a, z, span] for z in range(planes)]
                falling = [None] * planes
                falling[planes - 1] = at_member[owner, slot, i, 1, pl.ds(row, 8)]
                for z in range(planes - 1, 0, -1):
                    falling[z - 1] = (falling[z] + source[z]) * decay
                rising = at_member[owner, slot, i, 0, pl.ds(row, 8)]
                for z in range(planes):
                    rising = rising * decay + source[z]
                    field[c, a, z, span] = (rising + falling[z]) * scale
            return 0

        lax.fori_loop(0, chips, body, 0)

    def potential(c, a, z):
        return times_x(times_y(along_y[...], field[c, a, z]), along_x[...]) * weights[a][c]

    def first_potential(c, g):
        for step in range(GROUP):
            z = g * GROUP + step
            field[c, 0, z] = potential(c, 0, z)

    def inverse(c, g):
        for step in range(GROUP):
            z = g * GROUP + step
            total = None
            for a in range(band_dev):
                value = field[c, 0, z] if a == 0 else potential(c, a, z)
                term = value * own[a, z]
                total = term if total is None else total + term
                mutual = value * part[c, z]
                out[a, z] = mutual if c == 0 else out[a, z] + mutual
            given[c, z] = total
        out_copy(c, g).start()

    def loop(first, last, body):
        def step(g, _):
            body(g)
            return 0

        lax.fori_loop(first, last, step, 0)

    def settle(a, c):
        member_wait(a, c)
        solve(c, a)

    late = 1 - core
    loop(0, groups, functools.partial(forward, 0))
    summarise(0, 0)
    summarise(1, 0)
    loop(0, groups - 2, functools.partial(forward, 1))

    @pl.when(core == 0)
    def _():
        owner_wait(0)
        combine(0)

    loop(groups - 2, groups, functools.partial(forward, 1))
    summarise(0, 1)

    @pl.when(core == 0)
    def _():
        resolve(0)
        send_back(0, 1)
        send_back(0, 0)

    summarise(1, 1)
    owner_wait(late)
    combine(late)
    resolve(late)
    send_back(late, 0)
    send_back(late, 1)
    settle(0, 0)
    loop(0, groups, functools.partial(first_potential, 0))

    @pl.when(core == 1)
    def _():
        owner_wait(1)
        combine(1)

    settle(1, 0)
    loop(0, 1, functools.partial(inverse, 0))

    @pl.when(core == 1)
    def _():
        resolve(1)
        send_back(1, 0)
        send_back(1, 1)

    loop(1, groups, functools.partial(inverse, 0))
    settle(0, 1)
    loop(0, groups, functools.partial(first_potential, 1))
    settle(1, 1)
    loop(0, groups, functools.partial(inverse, 1))

    for c in range(band_dev):
        for g in range(groups):
            in_copy(c, g).wait_send()
            out_copy(c, g).wait_send()
            out_copy(c, g).wait_recv()
        half_copy(c).wait_send()
        for a in range(band_dev):
            for j in range(1, chips):
                owner_copy(a, c, j).wait_send()
            _, owner = pair(core, a, c)
            pl.when(core != owner)(owner_copy(a, c, 0).wait_send)
        for other_core in range(CORES):
            for j in range(1 - other_core, chips):
                member_copy(c, other_core, j).wait_send()


def solution(mesh):
    bands, slabs = mesh.shape["band"], mesh.shape["slab"]

    def local(orbitals, plan):
        band_dev, planes, rows, points = orbitals.shape
        members = slabs // HALVES
        chips = members // CORES
        chunk = rows // chips
        groups = planes // GROUP
        table_x, table_y, modes = constants(planes, planes * slabs, rows, points)
        plan = jnp.transpose(plan, (1, 2, 0))
        operands = (plan, orbitals, table_x, table_y, modes)
        f32 = jnp.float32
        field = pltpu.VMEM((band_dev, planes, rows, points), f32)
        edge = pltpu.VMEM((band_dev, chunk, points), f32)

        def semaphores(*shape):
            return [pltpu.SemaphoreType.DMA(shape)] * 2

        kept, taken = pl.pallas_call(
            functools.partial(kernel, bands, slabs),
            out_shape=[jax.ShapeDtypeStruct(orbitals.shape, f32)] * 2,
            in_specs=[pl.BlockSpec(memory_space=pltpu.HBM)] * 5,
            out_specs=[pl.BlockSpec(memory_space=pltpu.VMEM)] * 2,
            scratch_shapes=[
                pltpu.SMEM(plan.shape, plan.dtype),
                field,
                pltpu.VMEM(table_x.shape, f32),
                pltpu.VMEM(table_y.shape, f32),
                pltpu.VMEM(modes.shape, f32),
                pltpu.VMEM((2 * points, 2 * points), jnp.bfloat16),
                pltpu.VMEM((2 * rows, rows), jnp.bfloat16),
                field,
                pltpu.VMEM((band_dev, band_dev, planes, rows, points), f32),
                field,
                pltpu.VMEM((band_dev, band_dev, chips, 2, chunk, points), f32),
                pltpu.VMEM((band_dev, members, 2, chunk, points), f32),
                pltpu.VMEM((band_dev, members, 2, chunk, points), f32),
                pltpu.VMEM((CORES, band_dev, chips, 2, chunk, points), f32),
                edge,
                edge,
                edge,
                pltpu.SemaphoreType.DMA((5,)),
                *semaphores(band_dev, groups),
                *semaphores(band_dev, band_dev, chips),
                *semaphores(band_dev),
                *semaphores(CORES, band_dev, chips),
                *semaphores(band_dev, groups),
            ],
            compiler_params=pltpu.CompilerParams(
                collective_id=0, has_side_effects=True, vmem_limit_bytes=40 * 2**20
            ),
            name="exchange",
        )(*[pltpu.with_memory_space_constraint(jnp.asarray(x), pltpu.HBM) for x in operands])
        return kept + taken

    in_specs = (P("band", "slab", None, None), P())
    out_specs = P("band", "slab", None, None)
    return jax.shard_map(local, mesh=mesh, in_specs=in_specs, out_specs=out_specs, check_vma=False)
```
